256 devices in a mesh: ctx: 32 (over z_lo, y, core), head: 8 (over z_hi, x).
Axes of the slice: x: 4, y: 4, z: 8 (z_hi: 2, z_lo: 4; z = z_hi * 4 + z_lo), core: 2. Of those that a mesh axis runs over, the one named last changes fastest.
Arguments:
- query_rows: bfloat16 [4096, 4096], P('ctx', 'head'), may hold values from -16 to 16
- key_head_rows: bfloat16 [4096, 1024], P('ctx', 'head'), may hold values from -8 to 8
- value_head_rows: bfloat16 [4096, 1024], P('ctx', 'head'), may hold values from -6 to 6
- positions: int32 [4096], P('ctx'), may hold values from 0 to 4095, each once
- residual: bfloat16 [4096, 4096], P('ctx', 'head'), may hold values from -0.75 to 0.75
- norm_gain: bfloat16 [4096], P('head'), may hold values from 0.099609375 to 1.8984375
- expert_ids: int32 [4096, 2], P('ctx'), may hold values from 0 to 7, all different within a row; in each aligned block of 128 rows (0 to 127, 128 to 255, ...) at most 36 rows name the same one
- gate_fixed: int32 [4096], P('ctx'), may hold values from 6554 to 58982
- w_gate: bfloat16 [4096, 114688], P(None, ('ctx', 'head')), may hold values from -0.09375 to 0.09375
- w_up: bfloat16 [4096, 114688], P(None, ('ctx', 'head')), may hold values from -0.09375 to 0.09375
- w_down: bfloat16 [114688, 4096], P(('ctx', 'head')), may hold values from -0.046875 to 0.046875
Outputs:
- mixed: bfloat16 [4096, 4096], P('ctx', 'head')
The draws below stay inside these ranges and needn't reach their ends.
Inputs may be any that keep to these rules, and one draw needn't show every extreme that they name: `expert_ids`: within each aligned block of 128 rows (the rows of one index of ctx) no expert is named more than 36 times, a bound that some block reaches; the two experts of a row differ. `positions`: each position of the window appears once.
All inputs are finite; a program needn't handle non-finite values.
Results may differ from the reference program's by a relative error of at most 0.023.
Values may be sent and summed in bfloat16 or wider, within the bound.
A program may use at most 128 MiB of HBM per device.

```python
import math
import jax
import jax.numpy as jnp
import numpy as np
from jax import lax

D = 4096
QUERY_HEADS = 32
KEY_VALUE_HEADS = 8
HEAD_SIZE = 128
FF = 14336
EXPERTS = 8
TOP = 2
TOK_DEV = 128
WINDOW_TOKENS = 4096
CAP = 36
FF_DEV = 448
ROWS_CAP = 1152


def draw_key_head_rows(key, part):
    key = jax.random.fold_in(key, 11)
    base_random_key = jax.random.fold_in(key, 0)
    base_matrix = jnp.clip(jax.random.normal(base_random_key, (WINDOW_TOKENS, KEY_VALUE_HEADS * HEAD_SIZE), jnp.float32), -6.0, 6.0)
    return base_matrix.astype(jnp.bfloat16)


def draw_query_rows(key, part):
    key = jax.random.fold_in(key, 23)
    base_random_key = jax.random.fold_in(key, 0)
    base_matrix = 1.5 * jnp.clip(jax.random.normal(base_random_key, (WINDOW_TOKENS, D), jnp.float32), -6.0, 6.0)
    return base_matrix.astype(jnp.bfloat16)


def touch_ends(drawn, stream_key, least, largest):
    index_at = [jax.random.randint(jax.random.fold_in(stream_key, axis), (), 0, length) for axis, length in enumerate(drawn.shape)]
    main_axis = drawn.shape.index(max(drawn.shape))
    next_to = index_at[:main_axis] + [(index_at[main_axis] + 1) % drawn.shape[main_axis]] + index_at[main_axis + 1:]
    return drawn.at[tuple(index_at)].set(least).at[tuple(next_to)].set(largest)


def levels(rng, shape, cuts, smallest, high):
    level, own = 1.0, jax.random.fold_in(rng, 6)
    for axis_at, blocks in cuts:
        draws = jnp.exp(jax.random.uniform(jax.random.fold_in(own, axis_at), (blocks,), jnp.float32, smallest / len(cuts), high / len(cuts)))
        level = level * jnp.repeat(draws, shape[axis_at] // blocks).reshape([-1 if axis == axis_at else 1 for axis in range(len(shape))])
    return level


def routed_block(key, own, number, rows, amount, top, limit, slope):
    order = jax.random.permutation(key, amount)
    heavy_load, common = portions_of(amount, rows * top, limit, slope, True), portions_of(amount, rows * top, limit, slope, False)
    places = jnp.arange(amount)

    def named(tallies, turn):
        used = int((tallies > 0).sum())
        fixed = max(1, used // 4)
        moved = fixed + (places - fixed + turn * (used - fixed)) % max(1, amount - fixed)
        return jnp.zeros((amount,), jnp.int32).at[order[jnp.where(places < fixed, places, moved)]].set(jnp.asarray(tallies, jnp.int32))

    tallies = jnp.where(number % 4 == 0, named(heavy_load, number // 4), named(common, number - number // 4 - 1))
    mixed = jax.random.permutation(jax.random.fold_in(own, 3), amount)
    source_of, receiver = mixed[0:amount // 2 * 2:2], mixed[1:amount // 2 * 2:2]
    room = jnp.minimum(tallies[source_of] - 1, limit - tallies[receiver]) // 2
    room = jnp.where((source_of == order[0]) | (receiver == order[0]) | (tallies[receiver] == 0), 0, jnp.maximum(room, 0))
    moved = jax.random.randint(jax.random.fold_in(own, 4), (amount // 2,), 0, 1 << 20) % (room + 1)
    tallies = tallies.at[source_of].add(-moved).at[receiver].add(moved)
    members = jnp.searchsorted(jnp.cumsum(tallies), jnp.arange(rows * top), side="right").astype(jnp.int32)
    grid = members.reshape(top, rows).T
    grid = grid[jax.random.permutation(jax.random.fold_in(own, 1), rows)]
    turn = jax.random.randint(jax.random.fold_in(own, 2), (rows, 1), 0, top)
    return jnp.take_along_axis(grid, (jnp.arange(top)[None, :] + turn) % top, axis=1)


def portions_of(count, total, most, slope, full):
    weights = [(1 << 20) // math.isqrt(rank ** slope) + 1 for rank in range(1, count + 1)]
    largest = most if full else min(most, max(-(-total // count), total * weights[0] // sum(weights)))
    least = 1 if total - largest >= count - 1 else 0
    counts, rest = [largest] + [least] * (count - 1), total - largest - least * (count - 1)
    while rest > 0:
        movable = [i for i in range(1, count) if counts[i] < largest] or [i for i in range(1, count) if counts[i] < most]
        mass, budget = sum([weights[i] for i in movable]), rest
        for i in movable:
            extra = min(most - counts[i], max(1, budget * weights[i] // mass), rest)
            counts[i] = counts[i] + extra
            rest = rest - extra
    return np.array(counts)


def normal_values(stream_key, dims, spread, bound, cuts=(), kind=jnp.bfloat16):
    level = levels(stream_key, dims, cuts, -0.22, 0.18) if cuts else 1.0
    array = jax.random.normal(stream_key, dims, jnp.float32) * spread * level
    return jnp.minimum(jnp.maximum(array, -bound), bound).astype(kind)


def setup_inputs(seed: int = 0) -> dict:
    key_of = jax.random.split(jax.random.key(seed), 12)
    query_rows = draw_query_rows(jax.random.fold_in(key_of[11], 71), 0)
    key_head_rows = draw_key_head_rows(jax.random.fold_in(key_of[11], 71), 0)
    value_head_rows = normal_values(key_of[2], (WINDOW_TOKENS, KEY_VALUE_HEADS * HEAD_SIZE), 1.0, 6.0, ((0, 32), (1, 8)))
    positions = jax.random.permutation(key_of[3], WINDOW_TOKENS).astype(jnp.int32)
    residual = normal_values(key_of[4], (WINDOW_TOKENS, D), 0.05, 0.75, ((0, 32), (1, 8)))
    norm_gain = jnp.clip(1.0 + 0.18 * jax.random.normal(key_of[5], (D,), jnp.float32), 0.099609375, 1.8984375).astype(jnp.bfloat16)
    expert_ids_keys = jax.random.split(jax.random.fold_in(key_of[6], 1), WINDOW_TOKENS // TOK_DEV)
    expert_ids_turns = jax.random.permutation(jax.random.fold_in(key_of[6], 3), WINDOW_TOKENS // TOK_DEV)
    expert_ids = jax.vmap(lambda own, number: routed_block(jax.random.fold_in(key_of[6], 2), own, number, TOK_DEV, EXPERTS, TOP, CAP, 1))(expert_ids_keys, expert_ids_turns).reshape((WINDOW_TOKENS, TOP))
    gate_fixed = touch_ends(jax.random.randint(key_of[7], (WINDOW_TOKENS,), 6554, 58983), jax.random.fold_in(key_of[7], 1), 6554, 58982).astype(jnp.int32)
    w_gate = normal_values(key_of[8], (D, EXPERTS * FF), D ** -0.5, 0.09375, ((1, 256),))
    w_up = normal_values(key_of[9], (D, EXPERTS * FF), D ** -0.5, 0.09375, ((1, 256),))
    w_down = normal_values(key_of[10], (EXPERTS * FF, D), FF ** -0.5, 0.046875, ((0, 256),))
    return {"query_rows": query_rows, "key_head_rows": key_head_rows, "value_head_rows": value_head_rows, "positions": positions, "residual": residual, "norm_gain": norm_gain, "expert_ids": expert_ids, "gate_fixed": gate_fixed, "w_gate": w_gate, "w_up": w_up, "w_down": w_down}


def attention_core(query_rows, key_head_rows, value_head_rows, positions):
    query_group_size = QUERY_HEADS // KEY_VALUE_HEADS
    q_stack = query_rows.reshape(WINDOW_TOKENS, QUERY_HEADS, HEAD_SIZE).transpose(1, 0, 2)
    key_stack = key_head_rows.reshape(WINDOW_TOKENS, KEY_VALUE_HEADS, HEAD_SIZE).transpose(1, 0, 2)
    value_stack = value_head_rows.reshape(WINDOW_TOKENS, KEY_VALUE_HEADS, HEAD_SIZE).transpose(1, 0, 2)
    visible = positions[None, :] <= positions[:, None]

    def one_head(head_index):
        kv_index = (head_index // query_group_size).astype(jnp.int32)
        q_head = lax.dynamic_index_in_dim(q_stack, head_index.astype(jnp.int32), 0, keepdims=False)
        k_head = lax.dynamic_index_in_dim(key_stack, kv_index, 0, keepdims=False)
        v_head = lax.dynamic_index_in_dim(value_stack, kv_index, 0, keepdims=False)
        scores = jnp.dot(q_head, k_head.T, preferred_element_type=jnp.float32) * HEAD_SIZE ** (-0.5)
        scores = jnp.where(visible, scores, -jnp.inf)
        row_max = lax.optimization_barrier(jnp.max(scores, axis=1, keepdims=True))
        exp_scores = jnp.exp(scores - row_max)
        row_total = lax.optimization_barrier(jnp.sum(exp_scores, axis=1, keepdims=True))
        weighted = jnp.dot(exp_scores.astype(jnp.bfloat16), v_head, preferred_element_type=jnp.float32)
        return (weighted / row_total).astype(jnp.bfloat16)
    heads_out = lax.map(one_head, jnp.arange(QUERY_HEADS, dtype=jnp.int32))
    return heads_out.transpose(1, 0, 2).reshape(WINDOW_TOKENS, D)

def reference(query_rows, key_head_rows, value_head_rows, positions, residual, norm_gain, expert_ids, gate_fixed, w_gate, w_up, w_down):
    attention = attention_core(query_rows, key_head_rows, value_head_rows, positions)
    stream = residual.astype(jnp.float32) + attention.astype(jnp.float32)
    mean_sq = lax.optimization_barrier(jnp.mean(stream * stream, axis=1, keepdims=True))
    normed = (stream * lax.rsqrt(mean_sq + 1e-05) * norm_gain.astype(jnp.float32)).astype(jnp.bfloat16)
    first_weight = gate_fixed.astype(jnp.float32) / 65536.0
    pair_weights = jnp.stack([first_weight, 1.0 - first_weight], axis=1)
    shard_count = FF // FF_DEV
    expert_mix = jnp.zeros((WINDOW_TOKENS, D), jnp.float32)
    for expert in range(EXPERTS):
        expert_hits = expert_ids == expert
        routed = jnp.any(expert_hits, axis=1)
        routed_order = jnp.argsort(jnp.where(routed, 0, 1).astype(jnp.int32), stable=True)[:ROWS_CAP]
        row_weight = lax.optimization_barrier(jnp.sum(jnp.where(expert_hits, pair_weights, 0.0), axis=1))[routed_order]
        routed_rows = normed[routed_order]
        gate_part = jnp.dot(routed_rows, w_gate[:, expert * FF:(expert + 1) * FF], preferred_element_type=jnp.float32)
        up_part = jnp.dot(routed_rows, w_up[:, expert * FF:(expert + 1) * FF], preferred_element_type=jnp.float32)
        hidden = (jax.nn.silu(gate_part) * up_part).astype(jnp.bfloat16)
        hidden_shards = hidden.reshape(ROWS_CAP, shard_count, FF_DEV).transpose(1, 0, 2)
        down_shards = w_down[expert * FF:(expert + 1) * FF].reshape(shard_count, FF_DEV, D)

        def add_shard(running, shard_pair):
            partial_rows = jnp.dot(shard_pair[0], shard_pair[1], preferred_element_type=jnp.float32).astype(jnp.bfloat16)
            partial_rows = lax.optimization_barrier(partial_rows)
            return (running + partial_rows.astype(jnp.float32), None)
        down_rows, _ = lax.scan(add_shard, jnp.zeros((ROWS_CAP, D), jnp.float32), (hidden_shards, down_shards))
        expert_mix = expert_mix.at[routed_order].add(row_weight[:, None] * down_rows)
    return (stream + expert_mix).astype(jnp.bfloat16)
```

```python
import jax
import jax.numpy as jnp
from jax import lax
from jax.experimental import pallas as pl
from jax.experimental.pallas import tpu as pltpu
from jax.sharding import PartitionSpec as P

MESH = pl.DeviceIdType.MESH
HEAD_SIZE = 128
CAP = 36
SLOT = 48
EXPERTS = 8
ROWS = 8 * CAP
HALF = 512
QUARTER = ROWS // 2
SCALE = HEAD_SIZE ** (-0.5)
F32 = jnp.float32
BF16 = jnp.bfloat16


class Sems:
    def __init__(self, send, recv):
        self.send, self.recv, self.used = send, recv, 0

    def take(self, count=1):
        at = self.used
        self.used += count
        return at


def dot(a, b):
    return jnp.dot(a, b, preferred_element_type=F32)


def kernel(
    q_ref, k_ref, v_ref, ints_ref, posrow_ref, resid_ref, gain_ref, wg_hbm, wu_hbm, wd_hbm,
    out_ref,
    kv, ssq, stream, pick, cw, gbuf, d1, xb, wg, wu, wd, accg, accu, hid, yb, rq, rh, rf, z, r2s, r2,
    send, recv, local,
):
    c, h = lax.axis_index("ctx"), lax.axis_index("head")
    core, y, zl = lax.rem(c, 2), lax.rem(lax.div(c, 2), 4), lax.div(c, 8)
    yl, yh = lax.rem(y, 2), lax.div(y, 2)
    zh, x = lax.div(h, 4), lax.rem(h, 4)

    def at(zl_=zl, yh_=yh, yl_=yl, core_=core, zh_=zh, x_=x):
        return (zl_ * 8 + (yh_ * 2 + yl_) * 2 + core_, zh_ * 4 + x_)

    right, left = at(x_=lax.rem(x + 1, 4)), at(x_=lax.rem(x + 3, 4))
    across, mate = at(yl_=1 - yl), at(core_=1 - core)
    sems = Sems(send, recv)

    def copy(src, dst, n, device):
        return pltpu.make_async_remote_copy(
            src_ref=src, dst_ref=dst, send_sem=send.at[n], recv_sem=recv.at[n],
            device_id=device, device_id_type=MESH,
        )

    def arrive(dst, n):
        copy(dst, dst, n, mate).wait_recv()

    started = []

    def push(src, dst, n, device):
        copy(src, dst, n, device).start()
        started.append((src, n))

    loads = [
        pltpu.make_async_copy(wg_hbm, wg, local.at[0]),
        pltpu.make_async_copy(wu_hbm, wu, local.at[1]),
        pltpu.make_async_copy(
            wd_hbm.at[:, pl.ds(pl.multiple_of(core * 2048, 128), 2048)], wd.at[0], local.at[2]
        ),
    ]
    for load in loads:
        load.start()

    kv[0, 0, 0:128, :] = k_ref[...]
    kv[0, 0, 128:256, :] = v_ref[...]
    pos = posrow_ref[...]
    pos_hi = lax.shift_right_logical(pos, 6).astype(F32)
    pos_lo = (pos & 63).astype(F32)
    row16 = lax.broadcasted_iota(jnp.int32, (16, 128), 0)
    kv[0, 0, 256:272, :] = jnp.where(row16 == 0, pos_hi, pos_lo).astype(BF16)

    barrier = pltpu.get_barrier_semaphore()
    me16 = zl * 4 + y
    me32 = ((zh * 4 + zl) * 2 + yh) * 2 + core

    def greet(device):
        pl.semaphore_signal(barrier, inc=1, device_id=device, device_id_type=MESH)

    def kv_peer(r):
        j = lax.rem(me16 + r, 16)
        return (lax.div(j, 4) * 8 + lax.rem(j, 4) * 2 + core, h)

    @pl.loop(1, 16)
    def _(r):
        greet(kv_peer(r))

    @pl.loop(1, 8)
    def _(r):
        greet((c, lax.rem(h + r, 8)))

    @pl.loop(1, 32)
    def _(r):
        j = lax.rem(me32 + r, 32)
        greet(
            at(
                zl_=lax.rem(lax.div(j, 4), 4),
                yh_=lax.rem(lax.div(j, 2), 2),
                core_=lax.rem(j, 2),
                zh_=lax.div(j, 16),
            )
        )

    pl.semaphore_wait(barrier, 15 + 7 + 31)

    kv_n, mate_n, wd_n = sems.take(16), sems.take(16), sems.take()

    @pl.loop(1, 16)
    def _(r):
        copy(kv.at[0, 0], kv.at[0, r], kv_n + r, kv_peer(r)).start()

    copy(kv.at[0, 0], kv.at[1, 0], mate_n, mate).start()
    other = pl.multiple_of((1 - core) * 2048, 128)
    wd_move = copy(wd_hbm.at[:, pl.ds(other, 2048)], wd.at[1], wd_n, mate)
    wd_move.start()

    ids0, ids1 = ints_ref[:, 0:1], ints_ref[:, 1:2]
    lane = lax.broadcasted_iota(jnp.int32, (128, 128), 1)
    below = lax.broadcasted_iota(jnp.int32, (128, 128), 0) > lane
    hit0, hit1 = lane == ids0, lane == ids1
    hits = jnp.where(hit0 | hit1, 1.0, 0.0).astype(BF16)
    ranks = dot(jnp.where(below, 1.0, 0.0).astype(BF16), hits)
    slot0 = ids0.astype(F32) * SLOT + jnp.sum(jnp.where(hit0, ranks, 0.0), axis=1, keepdims=True)
    slot1 = ids1.astype(F32) * SLOT + jnp.sum(jnp.where(hit1, ranks, 0.0), axis=1, keepdims=True)
    places = lax.broadcasted_iota(jnp.int32, (128, EXPERTS * SLOT), 1).astype(F32)
    at0, at1 = places == slot0, places == slot1
    pick[...] = jnp.where(at0 | at1, 1.0, 0.0).astype(BF16)
    first = ints_ref[:, 2:3].astype(F32) / 65536.0
    weights = jnp.where(at0, first, 0.0) + jnp.where(at1, 1.0 - first, 0.0)
    coarse = weights.astype(BF16)
    cw[0] = coarse
    cw[1] = (weights - coarse.astype(F32)).astype(BF16)

    q = jnp.concatenate([q_ref[:, 128 * i : 128 * i + 128] for i in range(4)], axis=0)
    q_pos = jnp.concatenate([ints_ref[:, 3:4].astype(F32)] * 4, axis=0)

    def attend(side, group, carry):
        top, total, acc = carry
        part = kv[side, pl.ds(group * 4, 4)]
        keys = part[:, 0:128, :].reshape(512, 128)
        values = part[:, 128:256, :].reshape(512, 128)
        places = part[:, 256:272, :].astype(F32)
        k_pos = jnp.concatenate(
            [places[i, 0:1, :] * 64.0 + places[i, 1:2, :] for i in range(4)], axis=1
        )
        scores = lax.dot_general(q, keys, (((1,), (1,)), ((), ())), preferred_element_type=F32)
        scores = jnp.where(k_pos <= q_pos, scores * SCALE, -1e30)
        new_top = jnp.maximum(top, jnp.max(scores, axis=1, keepdims=True))
        keep = jnp.exp(top - new_top)
        probs = jnp.exp(scores - new_top)
        total = total * keep + jnp.sum(probs, axis=1, keepdims=True)
        acc = acc * keep + dot(probs.astype(BF16), values)
        return new_top, total, acc

    def own_side(group, carry):
        for i in range(4):
            r = group * 4 + i

            @pl.when(r > 0)
            def _(r=r):
                arrive(kv.at[0, r], kv_n + r)
                copy(kv.at[0, r], kv.at[1, r], mate_n + r, mate).start()

        return attend(0, group, carry)

    def mate_side(group, carry):
        for i in range(4):
            r = group * 4 + i
            arrive(kv.at[1, r], mate_n + r)
        return attend(1, group, carry)

    carry = (jnp.full((512, 1), -1e30, F32), jnp.zeros((512, 1), F32), jnp.zeros((512, 128), F32))
    carry = lax.fori_loop(0, 4, own_side, carry)
    _, total, acc = lax.fori_loop(0, 4, mate_side, carry)
    att = (acc / total).astype(BF16).astype(F32)
    att = jnp.concatenate([att[128 * i : 128 * i + 128] for i in range(4)], axis=1)
    flow = resid_ref[...].astype(F32) + att
    stream[...] = flow

    own_sq = jnp.sum(flow * flow, axis=1, keepdims=True)
    ssq[0] = jnp.transpose(jnp.broadcast_to(own_sq, (128, 128)))[0:8, :]
    ssq_n = sems.take(8)

    @pl.loop(1, 8)
    def _(r):
        copy(ssq.at[0], ssq.at[r], ssq_n + r, (c, lax.rem(h + r, 8))).start()

    @pl.loop(1, 8)
    def _(r):
        arrive(ssq.at[r], ssq_n + r)

    all_sq = jnp.sum(ssq[...], axis=0)
    all_sq = jnp.transpose(jnp.concatenate([all_sq] * 16, axis=0))[:, 0:1]
    normed = flow * lax.rsqrt(all_sq / 4096.0 + 1e-05) * gain_ref[...].astype(F32)
    rows = lax.dot_general(
        pick[...], normed.astype(BF16), (((0,), (0,)), ((), ())), preferred_element_type=F32
    ).astype(BF16)
    gbuf[...] = rows.reshape(EXPERTS, SLOT, HALF)

    d1_n = sems.take(16)
    me8 = zl * 2 + yh
    mine = zh * 8 + me8

    @pl.loop(1, 16)
    def _(r):
        j = lax.rem(mine + r, 16)
        e = lax.rem(j, 8)
        device = at(zl_=lax.div(e, 2), yh_=lax.rem(e, 2), zh_=lax.div(j, 8))
        copy(gbuf.at[e], d1.at[zh, me8], d1_n + r, device).start()

    d1[zh, me8] = gbuf[me8]

    @pl.loop(1, 16)
    def _(r):
        j = lax.rem(mine + 16 - r, 16)
        arrive(d1.at[lax.div(j, 8), lax.rem(j, 8)], d1_n + r)

    tight = lax.broadcasted_iota(jnp.int32, (ROWS, 8 * SLOT), 0)
    wide = lax.broadcasted_iota(jnp.int32, (ROWS, 8 * SLOT), 1)
    block = sum([jnp.where(tight >= CAP * i, 1, 0) for i in range(1, 8)])
    compact = jnp.where(wide == tight + block * (SLOT - CAP), 1.0, 0.0).astype(BF16)
    for i in range(2):
        xb[0, 0, 0, i] = dot(compact, d1[i].reshape(8 * SLOT, HALF)).astype(BF16)

    got = {}

    def relay(src, way, rows_of=None):
        side, dy, dx, i = src
        device, to = {
            "r": (right, (0, dy, (dx + 3) % 4, i)),
            "l": (left, (0, dy, (dx + 1) % 4, i)),
            "y": (across, (0, 1 - dy, dx, i)),
            "m": (mate, (1, dy, dx, i)),
        }[way]
        n = sems.take()
        part, there = xb.at[src], xb.at[to]
        if rows_of is not None:
            part = part.at[pl.ds(rows_of * QUARTER, QUARTER)]
            there = there.at[pl.ds(rows_of * QUARTER, QUARTER)]
        push(part, there, n, device)
        got[(*to, rows_of)] = (there, n)

    def landed(slot, rows_of=None):
        there, n = got[(*slot, rows_of)]
        arrive(there, n)

    for load in loads[:2]:
        load.wait()
    accg[...] = jnp.zeros_like(accg)
    accu[...] = jnp.zeros_like(accu)

    def multiply(side, dy, dx):
        xs = lax.rem(x + dx, 4)
        low = pl.ds(pl.multiple_of(xs * HALF, HALF), HALF)
        high = pl.ds(pl.multiple_of(2048 + xs * HALF, HALF), HALF)
        a, b = xb[side, dy, dx, 0], xb[side, dy, dx, 1]
        accg[side, dy] += dot(a, wg[low, :]) + dot(b, wg[high, :])
        accu[side, dy] += dot(a, wu[low, :]) + dot(b, wu[high, :])

    own = [(0, 0, 0, 0), (0, 0, 0, 1)]
    relay(own[0], "r"), relay(own[1], "l"), relay(own[0], "y")
    relay(own[1], "r"), relay(own[0], "l"), relay(own[1], "y")
    relay(own[0], "m"), relay(own[1], "m")
    multiply(0, 0, 0)
    landed((0, 0, 3, 0)), relay((0, 0, 3, 0), "r")
    landed((0, 0, 1, 1)), relay((0, 0, 1, 1), "l"), relay((0, 0, 1, 1), "y")
    landed((0, 1, 0, 0)), relay((0, 1, 0, 0), "r"), relay((0, 1, 0, 0), "l")
    landed((0, 0, 3, 1)), relay((0, 0, 3, 1), "y")
    landed((0, 0, 1, 0)), landed((0, 1, 0, 1))
    for slot in ((0, 3), (0, 1), (1, 0)):
        for i in range(2):
            relay((0, *slot, i), "m")
    landed((1, 0, 0, 0)), landed((1, 0, 0, 1))
    multiply(1, 0, 0)
    multiply(0, 0, 3)
    landed((0, 0, 2, 1)), relay((0, 0, 2, 1), "y"), relay((0, 0, 2, 1), "m")
    landed((0, 1, 3, 0)), relay((0, 1, 3, 0), "r", 0), relay((0, 1, 3, 0), "m")
    landed((0, 1, 1, 0)), relay((0, 1, 1, 0), "l", 1), relay((0, 1, 1, 0), "m")
    landed((0, 0, 2, 0)), relay((0, 0, 2, 0), "m")
    multiply(0, 0, 1)
    multiply(0, 1, 0)
    multiply(0, 0, 2)
    for slot in ((0, 3), (0, 1), (1, 0)):
        landed((1, *slot, 0)), landed((1, *slot, 1))
        multiply(1, *slot)
    landed((0, 1, 1, 1)), relay((0, 1, 1, 1), "m")
    landed((0, 1, 3, 1)), relay((0, 1, 3, 1), "m")
    multiply(0, 1, 1)
    multiply(0, 1, 3)
    landed((1, 0, 2, 0)), landed((1, 0, 2, 1))
    multiply(1, 0, 2)
    landed((0, 1, 2, 0), 0), landed((0, 1, 2, 0), 1), relay((0, 1, 2, 0), "m")
    landed((0, 1, 2, 1)), relay((0, 1, 2, 1), "m")
    multiply(0, 1, 2)
    for slot in ((1, 1), (1, 3), (1, 2)):
        landed((1, *slot, 0)), landed((1, *slot, 1))
        multiply(1, *slot)

    hid_n = {}
    for side, dy in ((0, 0), (1, 0), (0, 1), (1, 1)):
        g = accg[side, dy]
        hid[0, side, dy] = (g / (1.0 + jnp.exp(-g)) * accu[side, dy]).astype(BF16)
        n = hid_n[1 - side, dy] = sems.take()
        push(hid.at[0, side, dy], hid.at[1, 1 - side, dy], n, mate)
    loads[2].wait()
    wd_move.wait()
    for (side, dy), n in hid_n.items():
        arrive(hid.at[1, side, dy], n)

    def down(dy, dx):
        columns = pl.ds(pl.multiple_of(lax.rem(x + dx, 4) * HALF, HALF), HALF)
        for i in range(2):
            yb[dy, dx, i] = (
                dot(hid[0, i, dy], wd[0, :, columns]) + dot(hid[1, i, dy], wd[1, :, columns])
            ).astype(BF16)

    def add(into, *terms):
        value = into[...].astype(F32)
        for ref, _ in terms:
            value += ref[...].astype(F32)
        into[...] = value.astype(BF16)

    def give(src, dst, device):
        n = sems.take()
        push(src, dst, n, device)
        return dst, n

    def wait_all(*terms):
        for ref, n in terms:
            arrive(ref, n)

    down(1, 2)
    from_y2 = give(yb.at[1, 2, 1], rh.at[0], across)
    from_r_q = give(yb.at[1, 2, 0, pl.ds(0, QUARTER)], rq.at[0], left)
    from_l_q = give(yb.at[1, 2, 0, pl.ds(QUARTER, QUARTER)], rq.at[1], right)
    down(0, 2)
    from_r_2 = give(yb.at[0, 2, 0], rh.at[1], left)
    down(1, 3)
    from_y_3 = give(yb.at[1, 3, 1], rh.at[2], across)
    down(1, 1)
    from_y_1 = give(yb.at[1, 1, 1], rh.at[3], across)
    wait_all(from_y2, from_r_q, from_l_q)
    add(yb.at[0, 2, 1], from_y2)
    from_l_2 = give(yb.at[0, 2, 1], rh.at[4], right)
    add(yb.at[1, 3, 0, pl.ds(0, QUARTER)], from_r_q)
    from_r_3 = give(yb.at[1, 3, 0], rh.at[5], left)
    add(yb.at[1, 1, 0, pl.ds(QUARTER, QUARTER)], from_l_q)
    from_l_1 = give(yb.at[1, 1, 0], rh.at[6], right)
    down(0, 1)
    last_l = [give(yb.at[0, 1, 0], rf.at[0, 0], right), None]
    down(1, 0)
    last_y = [None, give(yb.at[1, 0, 1], rf.at[1, 1], across)]
    down(0, 3)
    wait_all(from_r_2)
    add(yb.at[0, 3, 0], from_r_2)
    last_r = [give(yb.at[0, 3, 0], rf.at[2, 0], left), None]
    wait_all(from_y_3)
    add(yb.at[0, 3, 1], from_y_3)
    last_r[1] = give(yb.at[0, 3, 1], rf.at[2, 1], left)
    wait_all(from_y_1, from_l_2)
    add(yb.at[0, 1, 1], from_y_1, from_l_2)
    last_l[1] = give(yb.at[0, 1, 1], rf.at[0, 1], right)
    wait_all(from_r_3, from_l_1)
    add(yb.at[1, 0, 0], from_r_3, from_l_1)
    last_y[0] = give(yb.at[1, 0, 0], rf.at[1, 0], across)
    down(0, 0)

    wide = lax.broadcasted_iota(jnp.int32, (8 * SLOT, ROWS), 0)
    tight = lax.broadcasted_iota(jnp.int32, (8 * SLOT, ROWS), 1)
    block = sum([jnp.where(tight >= CAP * i, 1, 0) for i in range(1, 8)])
    spread = jnp.where(wide == tight + block * (SLOT - CAP), 1.0, 0.0).astype(BF16)
    r2_n = sems.take(16)
    r2_s = sems.take(16)

    def back(i, r):
        s = lax.rem(me8 + r, 8)
        device = at(
            zl_=lax.div(s, 2),
            yh_=lax.rem(s, 2),
            core_=core if i == 0 else 1 - core,
            zh_=core,
        )
        return pltpu.make_async_remote_copy(
            src_ref=r2s.at[i, s], dst_ref=r2.at[zh, me8],
            send_sem=send.at[r2_s + 8 * i + r], recv_sem=recv.at[r2_n + zh * 8 + me8],
            device_id=device, device_id_type=MESH,
        )

    for i in range(2):
        wait_all(last_l[i], last_r[i], last_y[i])
        value = (
            yb[0, 0, i].astype(F32)
            + rf[0, i].astype(F32)
            + rf[1, i].astype(F32)
            + rf[2, i].astype(F32)
        ).astype(BF16)
        r2s[i] = dot(spread, value).astype(BF16).reshape(8, SLOT, HALF)
        if i == 0:

            @pl.when(core == zh)
            def _():
                r2[zh, me8] = r2s[0, me8]

            @pl.when(core != zh)
            def _():
                back(0, 0).start()

            pl.loop(1, 8)(lambda r: back(0, r).start())
        else:
            pl.loop(0, 8)(lambda r: back(1, r).start())

    @pl.loop(1, 16)
    def _(r):
        j = lax.rem(mine + r, 16)
        arrive(r2.at[lax.div(j, 8), lax.rem(j, 8)], r2_n + j)

    @pl.when(core != zh)
    def _():
        arrive(r2.at[zh, me8], r2_n + mine)

    mix = stream[...]
    for i in range(2):
        back_rows = r2[i].reshape(8 * SLOT, HALF)
        mix += dot(cw[0], back_rows) + dot(cw[1], back_rows)
    out_ref[...] = mix.astype(BF16)

    for src, n in started:
        copy(src, src, n, mate).wait_send()

    @pl.loop(1, 16)
    def _(r):
        copy(kv.at[0, 0], kv.at[0, 0], kv_n + r, mate).wait_send()
        copy(gbuf.at[0], gbuf.at[0], d1_n + r, mate).wait_send()

    @pl.loop(0, 16)
    def _(r):
        copy(kv.at[0, 0], kv.at[0, 0], mate_n + r, mate).wait_send()

    @pl.loop(1, 8)
    def _(r):
        copy(ssq.at[0], ssq.at[0], ssq_n + r, mate).wait_send()

    @pl.when(core != zh)
    def _():
        back(0, 0).wait_send()

    pl.loop(1, 8)(lambda r: back(0, r).wait_send())
    pl.loop(0, 8)(lambda r: back(1, r).wait_send())
    print("semaphores", sems.used) if False else None


SEMS = 192


def body(
    query_rows, key_head_rows, value_head_rows, positions, residual, norm_gain, expert_ids,
    gate_fixed, w_gate, w_up, w_down,
):
    ints = jnp.concatenate([expert_ids, gate_fixed[:, None], positions[:, None]], axis=1)
    vmem = pl.BlockSpec(memory_space=pltpu.VMEM)
    hbm = pl.BlockSpec(memory_space=pl.ANY)
    return pl.pallas_call(
        kernel,
        out_shape=jax.ShapeDtypeStruct(residual.shape, BF16),
        in_specs=[vmem] * 7 + [hbm] * 3,
        out_specs=vmem,
        scratch_shapes=[
            pltpu.VMEM((2, 16, 272, 128), BF16),
            pltpu.VMEM((8, 8, 128), F32),
            pltpu.VMEM((128, HALF), F32),
            pltpu.VMEM((128, EXPERTS * SLOT), BF16),
            pltpu.VMEM((2, 128, EXPERTS * SLOT), BF16),
            pltpu.VMEM((EXPERTS, SLOT, HALF), BF16),
            pltpu.VMEM((2, 8, SLOT, HALF), BF16),
            pltpu.VMEM((2, 2, 4, 2, ROWS, HALF), BF16),
            pltpu.VMEM(w_gate.shape, BF16),
            pltpu.VMEM(w_up.shape, BF16),
            pltpu.VMEM((2, w_down.shape[0], 2048), BF16),
            pltpu.VMEM((2, 2, ROWS, w_gate.shape[1]), F32),
            pltpu.VMEM((2, 2, ROWS, w_gate.shape[1]), F32),
            pltpu.VMEM((2, 2, 2, ROWS, w_gate.shape[1]), BF16),
            pltpu.VMEM((2, 4, 2, ROWS, HALF), BF16),
            pltpu.VMEM((2, QUARTER, HALF), BF16),
            pltpu.VMEM((7, ROWS, HALF), BF16),
            pltpu.VMEM((3, 2, ROWS, HALF), BF16),
            pltpu.VMEM((8, 128), F32),
            pltpu.VMEM((2, 8, SLOT, HALF), BF16),
            pltpu.VMEM((2, 8, SLOT, HALF), BF16),
            pltpu.SemaphoreType.DMA((SEMS,)),
            pltpu.SemaphoreType.DMA((SEMS,)),
            pltpu.SemaphoreType.DMA((3,)),
        ],
        compiler_params=pltpu.CompilerParams(
            collective_id=0, has_side_effects=True, vmem_limit_bytes=60 * 2**20
        ),
        cost_estimate=pl.CostEstimate(
            flops=14 * 10**9, bytes_accessed=12 * 10**6, transcendentals=3 * 10**6
        ),
    )(
        query_rows, key_head_rows, value_head_rows, ints, positions.reshape(1, -1), residual,
        norm_gain.reshape(1, -1), w_gate, w_up, w_down,
    )


def solution(mesh):
    in_specs = (
        P("ctx", "head"),
        P("ctx", "head"),
        P("ctx", "head"),
        P("ctx"),
        P("ctx", "head"),
        P("head"),
        P("ctx", None),
        P("ctx"),
        P(None, ("ctx", "head")),
        P(None, ("ctx", "head")),
        P(("ctx", "head"), None),
    )
    out_specs = P("ctx", "head")
    return jax.shard_map(body, mesh=mesh, in_specs=in_specs, out_specs=out_specs, check_vma=False)
```

```python
import jax
import jax.numpy as jnp
from jax import lax
from jax.experimental import pallas as pl
from jax.experimental.pallas import tpu as pltpu
from jax.sharding import PartitionSpec as P

MESH = pl.DeviceIdType.MESH
HEAD_SIZE = 128
CAP = 36
SLOT = 48
EXPERTS = 8
ROWS = 8 * CAP
HALF = 512
QUARTER = ROWS // 2
SCALE = HEAD_SIZE ** (-0.5)
F32 = jnp.float32
BF16 = jnp.bfloat16


class Sems:
    def __init__(self, send, recv):
        self.send, self.recv, self.used = send, recv, 0

    def take(self, count=1):
        at = self.used
        self.used += count
        return at


def dot(a, b):
    return jnp.dot(a, b, preferred_element_type=F32)


def dot_t(a, b):
    return lax.dot_general(a, b, (((1,), (1,)), ((), ())), preferred_element_type=F32)


def kernel(
    q_ref, k_ref, v_ref, ids_ref, gate_ref, pos_ref, resid_ref, gain_ref, wg_hbm, wu_hbm, wd_hbm,
    out_ref,
    kv, ssq, stream, pick, cw, gbuf, d1, xb, wg, wu, wd, accg, accu, hid, yb, rq, rh, rf, r2s, r2,
    send, recv, local,
):
    c, h = lax.axis_index("ctx"), lax.axis_index("head")
    core, y, zl = lax.rem(c, 2), lax.rem(lax.div(c, 2), 4), lax.div(c, 8)
    yl, yh = lax.rem(y, 2), lax.div(y, 2)
    zh, x = lax.div(h, 4), lax.rem(h, 4)

    def at(zl_=zl, yh_=yh, yl_=yl, core_=core, zh_=zh, x_=x):
        return (zl_ * 8 + (yh_ * 2 + yl_) * 2 + core_, zh_ * 4 + x_)

    def kin(zl_=zl, yh_=yh, core_=core, zh_=zh):
        return at(zl_=zl_, yh_=yh_, yl_=lax.rem(yl + yh + yh_, 2), core_=core_, zh_=zh_)

    right, left = at(x_=lax.rem(x + 1, 4)), at(x_=lax.rem(x + 3, 4))
    across, mate = at(yl_=1 - yl), at(core_=1 - core)
    up, under = (
        at(yh_=lax.div(lax.rem(y + i, 4), 2), yl_=lax.rem(y + i, 2)) for i in (1, 3)
    )
    sems = Sems(send, recv)

    def copy(src, dst, n, device):
        return pltpu.make_async_remote_copy(
            src_ref=src, dst_ref=dst, send_sem=send.at[n], recv_sem=recv.at[n],
            device_id=device, device_id_type=MESH,
        )

    def arrive(dst, n):
        copy(dst, dst, n, mate).wait_recv()

    started = []

    def push(src, dst, n, device):
        copy(src, dst, n, device).start()
        started.append((src, n))

    loads = [
        pltpu.make_async_copy(wg_hbm, wg, local.at[0]),
        pltpu.make_async_copy(wu_hbm, wu, local.at[1]),
        pltpu.make_async_copy(
            wd_hbm.at[:, pl.ds(pl.multiple_of(core * 2048, 128), 2048)], wd.at[0], local.at[2]
        ),
    ]
    for load in loads:
        load.start()

    kv[0, 0, 0, 0:128, :] = k_ref[...]
    kv[0, 0, 0, 128:256, :] = v_ref[...]
    pos = pos_ref[...]
    pos_hi = lax.shift_right_logical(pos, 6).astype(F32)
    pos_lo = (pos & 63).astype(F32)
    row16 = lax.broadcasted_iota(jnp.int32, (16, 128), 0)
    kv[0, 0, 0, 256:272, :] = jnp.where(row16 == 0, pos_hi, pos_lo).astype(BF16)

    barrier = pltpu.get_barrier_semaphore()
    me32 = ((zh * 4 + zl) * 2 + yh) * 2 + core

    def greet(device):
        pl.semaphore_signal(barrier, inc=1, device_id=device, device_id_type=MESH)

    @pl.loop(1, 8)
    def _(r):
        greet((c, lax.rem(h + r, 8)))

    @pl.loop(1, 32)
    def _(r):
        j = lax.rem(me32 + r, 32)
        greet(
            kin(
                zl_=lax.rem(lax.div(j, 4), 4),
                yh_=lax.rem(lax.div(j, 2), 2),
                core_=lax.rem(j, 2),
                zh_=lax.div(j, 16),
            )
        )

    greet(up), greet(under)
    pl.semaphore_wait(barrier, 7 + 31 + 2)

    kv_n, kv_half, mate_n, wd_n = sems.take(16), sems.take(4), sems.take(16), sems.take()

    def kv_mate(dy, dz):
        n = mate_n + dy * 4 + dz
        copy(kv.at[0, dy, dz], kv.at[1, dy, dz], n, mate).start()

    def kv_round(dz):
        copy(kv.at[0, 0, dz], kv.at[0, 3, dz], kv_n + 12 + dz, up).start()
        copy(kv.at[0, 0, dz], kv.at[0, 1, dz], kv_n + 4 + dz, under).start()

    for dz in (3, 1, 2):
        copy(kv.at[0, 0, 0], kv.at[0, 0, dz], kv_n + dz, at(zl_=lax.rem(zl + 4 - dz, 4))).start()
    kv_round(0)
    kv_mate(0, 0)
    other = pl.multiple_of((1 - core) * 2048, 128)
    wd_move = copy(wd_hbm.at[:, pl.ds(other, 2048)], wd.at[1], wd_n, mate)
    wd_move.start()

    numbers = jnp.concatenate(
        [ids_ref[...].astype(F32), gate_ref[...].astype(F32), pos.astype(F32)] * 32, axis=0
    )
    numbers = jnp.transpose(numbers)
    ids0, ids1, gates, places = (numbers[:, i : i + 1] for i in range(4))
    lane = lax.broadcasted_iota(jnp.int32, (128, 128), 1)
    below = lax.broadcasted_iota(jnp.int32, (128, 128), 0) > lane
    hit0, hit1 = lane.astype(F32) == ids0, lane.astype(F32) == ids1
    hits = jnp.where(hit0 | hit1, 1.0, 0.0).astype(BF16)
    ranks = dot(jnp.where(below, 1.0, 0.0).astype(BF16), hits)
    slot0 = ids0 * SLOT + jnp.sum(jnp.where(hit0, ranks, 0.0), axis=1, keepdims=True)
    slot1 = ids1 * SLOT + jnp.sum(jnp.where(hit1, ranks, 0.0), axis=1, keepdims=True)
    slots = lax.broadcasted_iota(jnp.int32, (128, EXPERTS * SLOT), 1).astype(F32)
    at0, at1 = slots == slot0, slots == slot1
    pick[...] = jnp.where(at0 | at1, 1.0, 0.0).astype(BF16)
    first = gates / 65536.0
    weights = jnp.where(at0, first, 0.0) + jnp.where(at1, 1.0 - first, 0.0)
    coarse = weights.astype(BF16)
    cw[0] = coarse
    cw[1] = (weights - coarse.astype(F32)).astype(BF16)

    q = jnp.concatenate([q_ref[:, 128 * i : 128 * i + 128] for i in range(4)], axis=0)
    q_pos = jnp.concatenate([places] * 4, axis=0)

    def attend(side, group, carry):
        top, total, acc = carry
        part = kv[side, group]
        keys = part[:, 0:128, :].reshape(512, 128)
        values = part[:, 128:256, :].reshape(512, 128)
        digits = part[:, 256:272, :].astype(F32)
        k_pos = jnp.concatenate(
            [digits[i, 0:1, :] * 64.0 + digits[i, 1:2, :] for i in range(4)], axis=1
        )
        scores = dot_t(q, keys)
        scores = jnp.where(k_pos <= q_pos, scores * SCALE, -1e30)
        new_top = jnp.maximum(top, jnp.max(scores, axis=1, keepdims=True))
        keep = jnp.exp(top - new_top)
        probs = jnp.exp(scores - new_top)
        total = total * keep + jnp.sum(probs, axis=1, keepdims=True)
        acc = acc * keep + dot(probs.astype(BF16), values)
        return new_top, total, acc

    early, late = pl.ds(0, 128), pl.ds(128, 144)

    def mate_side(step, carry):
        dy = step ^ lax.shift_right_logical(step, 1)
        for dz in range(4):
            arrive(kv.at[1, dy, dz], mate_n + dy * 4 + dz)
        return attend(1, dy, carry)

    carry = (jnp.full((512, 1), -1e30, F32), jnp.zeros((512, 1), F32), jnp.zeros((512, 128), F32))
    for dz in (1, 3, 2):
        arrive(kv.at[0, 0, dz], kv_n + dz)
        kv_round(dz)
        kv_mate(0, dz)
    carry = attend(0, 0, carry)
    for dz in (0, 1, 3, 2):
        arrive(kv.at[0, 3, dz], kv_n + 12 + dz)
        copy(kv.at[0, 3, dz, early], kv.at[0, 2, dz, early], kv_n + 8 + dz, up).start()
        kv_mate(3, dz)
        arrive(kv.at[0, 1, dz], kv_n + 4 + dz)
        copy(kv.at[0, 1, dz, late], kv.at[0, 2, dz, late], kv_half + dz, under).start()
        kv_mate(1, dz)
    carry = attend(0, 1, carry)
    carry = attend(0, 3, carry)
    for dz in (0, 1, 3, 2):
        arrive(kv.at[0, 2, dz, early], kv_n + 8 + dz)
        arrive(kv.at[0, 2, dz, late], kv_half + dz)
        kv_mate(2, dz)
    carry = attend(0, 2, carry)
    _, total, acc = lax.fori_loop(0, 4, mate_side, carry)
    att = (acc / total).astype(BF16).astype(F32)
    att = jnp.concatenate([att[128 * i : 128 * i + 128] for i in range(4)], axis=1)
    flow = resid_ref[...].astype(F32) + att
    stream[...] = flow

    own_sq = jnp.sum(flow * flow, axis=1, keepdims=True)
    ssq[0] = jnp.transpose(jnp.broadcast_to(own_sq, (128, 128)))[0:8, :]
    ssq_n = sems.take(8)

    @pl.loop(1, 8)
    def _(r):
        copy(ssq.at[0], ssq.at[r], ssq_n + r, (c, lax.rem(h + r, 8))).start()

    @pl.loop(1, 8)
    def _(r):
        arrive(ssq.at[r], ssq_n + r)

    all_sq = jnp.sum(ssq[...], axis=0)
    all_sq = jnp.transpose(jnp.concatenate([all_sq] * 16, axis=0))[:, 0:1]
    normed = flow * lax.rsqrt(all_sq / 4096.0 + 1e-05) * gain_ref[...].astype(F32)
    rows = lax.dot_general(
        pick[...], normed.astype(BF16), (((0,), (0,)), ((), ())), preferred_element_type=F32
    ).astype(BF16)
    gbuf[...] = rows.reshape(EXPERTS, SLOT, HALF)

    d1_n = sems.take(16)
    me8 = zl * 2 + yh
    mine = zh * 8 + me8

    def dispatch(i, r):
        e = lax.rem(me8 + r, 8)
        device = kin(zl_=lax.div(e, 2), yh_=lax.rem(e, 2), zh_=zh if i == 0 else 1 - zh)
        copy(gbuf.at[e], d1.at[i, me8], d1_n + 8 * i + r, device).start()

    pl.loop(1, 8)(lambda r: dispatch(0, r))
    pl.loop(0, 8)(lambda r: dispatch(1, r))
    d1[0, me8] = gbuf[me8]

    def dispatched(i, r):
        arrive(d1.at[i, lax.rem(me8 + 8 - r, 8)], d1_n + 8 * i + r)

    tight = lax.broadcasted_iota(jnp.int32, (ROWS, 8 * SLOT), 0)
    wide = lax.broadcasted_iota(jnp.int32, (ROWS, 8 * SLOT), 1)
    block = sum([jnp.where(tight >= CAP * i, 1, 0) for i in range(1, 8)])
    compact = jnp.where(wide == tight + block * (SLOT - CAP), 1.0, 0.0).astype(BF16)

    def compacted(i):
        xb[0, 0, 0, i] = dot(compact, d1[i].reshape(8 * SLOT, HALF)).astype(BF16)

    got = {}

    def relay(src, way, rows_of=None):
        side, dy, dx, i = src
        device, to = {
            "r": (right, (0, dy, (dx + 3) % 4, i)),
            "l": (left, (0, dy, (dx + 1) % 4, i)),
            "y": (across, (0, 1 - dy, dx, i)),
            "m": (mate, (1, dy, dx, i)),
        }[way]
        n = sems.take()
        part, there = xb.at[src], xb.at[to]
        if rows_of is not None:
            part = part.at[pl.ds(rows_of * QUARTER, QUARTER)]
            there = there.at[pl.ds(rows_of * QUARTER, QUARTER)]
        push(part, there, n, device)
        got[(*to, rows_of)] = (there, n)

    def landed(slot, rows_of=None):
        there, n = got[(*slot, rows_of)]
        arrive(there, n)

    def multiply(side, dy, dx):
        xs = lax.rem(x + dx, 4)
        low = pl.ds(pl.multiple_of((zh * 4 + xs) * HALF, HALF), HALF)
        high = pl.ds(pl.multiple_of(((1 - zh) * 4 + xs) * HALF, HALF), HALF)
        a, b = xb[side, dy, dx, 0], xb[side, dy, dx, 1]
        accg[side, dy] += dot_t(a, wg[:, low]) + dot_t(b, wg[:, high])
        accu[side, dy] += dot_t(a, wu[:, low]) + dot_t(b, wu[:, high])

    own = [(0, 0, 0, 0), (0, 0, 0, 1)]
    pl.loop(1, 8)(lambda r: dispatched(0, r))
    compacted(0)
    relay(own[0], "r"), relay(own[0], "l"), relay(own[0], "y"), relay(own[0], "m")
    for load in loads[:2]:
        load.wait()
    accg[...] = jnp.zeros_like(accg)
    accu[...] = jnp.zeros_like(accu)
    pl.loop(0, 8)(lambda r: dispatched(1, r))
    compacted(1)
    relay(own[1], "l"), relay(own[1], "r"), relay(own[1], "y"), relay(own[1], "m")
    landed((0, 0, 3, 0)), relay((0, 0, 3, 0), "r")
    landed((0, 1, 0, 0)), relay((0, 1, 0, 0), "r"), relay((0, 1, 0, 0), "l")
    multiply(0, 0, 0)
    landed((0, 0, 1, 1)), relay((0, 0, 1, 1), "l"), relay((0, 0, 1, 1), "y")
    landed((0, 0, 3, 1)), relay((0, 0, 3, 1), "y")
    landed((0, 0, 1, 0)), landed((0, 1, 0, 1))
    for slot in ((0, 3), (0, 1), (1, 0)):
        for i in range(2):
            relay((0, *slot, i), "m")
    landed((1, 0, 0, 0)), landed((1, 0, 0, 1))
    multiply(1, 0, 0)
    multiply(0, 0, 3)
    landed((0, 0, 2, 1)), relay((0, 0, 2, 1), "y"), relay((0, 0, 2, 1), "m")
    landed((0, 1, 3, 0)), relay((0, 1, 3, 0), "r", 0), relay((0, 1, 3, 0), "m")
    landed((0, 1, 1, 0)), relay((0, 1, 1, 0), "l", 1), relay((0, 1, 1, 0), "m")
    landed((0, 0, 2, 0)), relay((0, 0, 2, 0), "m")
    multiply(0, 0, 1)
    multiply(0, 1, 0)
    multiply(0, 0, 2)
    for slot in ((0, 3), (0, 1), (1, 0)):
        landed((1, *slot, 0)), landed((1, *slot, 1))
        multiply(1, *slot)
    landed((0, 1, 1, 1)), relay((0, 1, 1, 1), "m")
    landed((0, 1, 3, 1)), relay((0, 1, 3, 1), "m")
    multiply(0, 1, 1)
    multiply(0, 1, 3)
    landed((1, 0, 2, 0)), landed((1, 0, 2, 1))
    multiply(1, 0, 2)
    landed((0, 1, 2, 0), 0), landed((0, 1, 2, 0), 1), relay((0, 1, 2, 0), "m")
    landed((0, 1, 2, 1)), relay((0, 1, 2, 1), "m")
    multiply(0, 1, 2)
    for slot in ((1, 1), (1, 3), (1, 2)):
        landed((1, *slot, 0)), landed((1, *slot, 1))
        multiply(1, *slot)

    hid_n = {}
    for side, dy in ((0, 0), (1, 0), (0, 1), (1, 1)):
        g = accg[side, dy]
        hid[0, side, dy] = (g / (1.0 + jnp.exp(-g)) * accu[side, dy]).astype(BF16)
        n = hid_n[1 - side, dy] = sems.take()
        push(hid.at[0, side, dy], hid.at[1, 1 - side, dy], n, mate)
    loads[2].wait()
    wd_move.wait()
    for (side, dy), n in hid_n.items():
        arrive(hid.at[1, side, dy], n)

    def down(dy, dx):
        columns = pl.ds(pl.multiple_of(lax.rem(x + dx, 4) * HALF, HALF), HALF)
        for i in range(2):
            yb[dy, dx, i] = (
                dot(hid[0, i, dy], wd[0, :, columns]) + dot(hid[1, i, dy], wd[1, :, columns])
            ).astype(BF16)

    def add(into, *terms):
        value = into[...].astype(F32)
        for ref, _ in terms:
            value += ref[...].astype(F32)
        into[...] = value.astype(BF16)

    def give(src, dst, device):
        n = sems.take()
        push(src, dst, n, device)
        return dst, n

    def wait_all(*terms):
        for ref, n in terms:
            arrive(ref, n)

    down(1, 2)
    from_y2 = give(yb.at[1, 2, 1], rh.at[0], across)
    from_r_q = give(yb.at[1, 2, 0, pl.ds(0, QUARTER)], rq.at[0], left)
    from_l_q = give(yb.at[1, 2, 0, pl.ds(QUARTER, QUARTER)], rq.at[1], right)
    down(0, 2)
    from_r_2 = give(yb.at[0, 2, 0], rh.at[1], left)
    down(1, 3)
    from_y_3 = give(yb.at[1, 3, 1], rh.at[2], across)
    down(1, 1)
    from_y_1 = give(yb.at[1, 1, 1], rh.at[3], across)
    wait_all(from_y2, from_r_q, from_l_q)
    add(yb.at[0, 2, 1], from_y2)
    from_l_2 = give(yb.at[0, 2, 1], rh.at[4], right)
    add(yb.at[1, 3, 0, pl.ds(0, QUARTER)], from_r_q)
    from_r_3 = give(yb.at[1, 3, 0], rh.at[5], left)
    add(yb.at[1, 1, 0, pl.ds(QUARTER, QUARTER)], from_l_q)
    from_l_1 = give(yb.at[1, 1, 0], rh.at[6], right)
    down(0, 1)
    last_l = [give(yb.at[0, 1, 0], rf.at[0, 0], right), None]
    down(1, 0)
    last_y = [None, give(yb.at[1, 0, 1], rf.at[1, 1], across)]
    down(0, 3)
    wait_all(from_r_2)
    add(yb.at[0, 3, 0], from_r_2)
    last_r = [give(yb.at[0, 3, 0], rf.at[2, 0], left), None]
    wait_all(from_y_3)
    add(yb.at[0, 3, 1], from_y_3)
    last_r[1] = give(yb.at[0, 3, 1], rf.at[2, 1], left)
    wait_all(from_y_1, from_l_2)
    add(yb.at[0, 1, 1], from_y_1, from_l_2)
    last_l[1] = give(yb.at[0, 1, 1], rf.at[0, 1], right)
    wait_all(from_r_3, from_l_1)
    add(yb.at[1, 0, 0], from_r_3, from_l_1)
    last_y[0] = give(yb.at[1, 0, 0], rf.at[1, 0], across)
    down(0, 0)

    wide = lax.broadcasted_iota(jnp.int32, (8 * SLOT, ROWS), 0)
    tight = lax.broadcasted_iota(jnp.int32, (8 * SLOT, ROWS), 1)
    block = sum([jnp.where(tight >= CAP * i, 1, 0) for i in range(1, 8)])
    spread = jnp.where(wide == tight + block * (SLOT - CAP), 1.0, 0.0).astype(BF16)
    r2_n = sems.take(16)
    r2_s = sems.take(16)

    def back(i, r):
        s = lax.rem(me8 + r, 8)
        device = kin(
            zl_=lax.div(s, 2), yh_=lax.rem(s, 2), core_=core if i == 0 else 1 - core, zh_=core
        )
        return pltpu.make_async_remote_copy(
            src_ref=r2s.at[i, s], dst_ref=r2.at[zh, me8],
            send_sem=send.at[r2_s + 8 * i + r], recv_sem=recv.at[r2_n + zh * 8 + me8],
            device_id=device, device_id_type=MESH,
        )

    for i in range(2):
        wait_all(last_l[i], last_r[i], last_y[i])
        value = (
            yb[0, 0, i].astype(F32)
            + rf[0, i].astype(F32)
            + rf[1, i].astype(F32)
            + rf[2, i].astype(F32)
        ).astype(BF16)
        r2s[i] = dot(spread, value).astype(BF16).reshape(8, SLOT, HALF)
        if i == 0:

            @pl.when(core == zh)
            def _():
                r2[zh, me8] = r2s[0, me8]

            @pl.when(core != zh)
            def _():
                back(0, 0).start()

            pl.loop(1, 8)(lambda r: back(0, r).start())
        else:
            pl.loop(0, 8)(lambda r: back(1, r).start())

    @pl.loop(1, 16)
    def _(r):
        j = lax.rem(mine + r, 16)
        arrive(r2.at[lax.div(j, 8), lax.rem(j, 8)], r2_n + j)

    @pl.when(core != zh)
    def _():
        arrive(r2.at[zh, me8], r2_n + mine)

    mix = stream[...]
    for i in range(2):
        back_rows = r2[i].reshape(8 * SLOT, HALF)
        mix += dot(cw[0], back_rows) + dot(cw[1], back_rows)
    out_ref[...] = mix.astype(BF16)

    for src, n in started:
        copy(src, src, n, mate).wait_send()

    @pl.loop(1, 16)
    def _(r):
        copy(gbuf.at[0], gbuf.at[0], d1_n + r, mate).wait_send()

    @pl.loop(0, 16)
    def _(r):
        copy(kv.at[0, 0, 0], kv.at[0, 0, 0], mate_n + r, mate).wait_send()

    for n in (*range(1, 8), *range(12, 16)):
        copy(kv.at[0, 0, 0], kv.at[0, 0, 0], kv_n + n, mate).wait_send()
    for n in range(4):
        copy(kv.at[0, 0, 0, early], kv.at[0, 0, 0, early], kv_n + 8 + n, mate).wait_send()
        copy(kv.at[0, 0, 0, late], kv.at[0, 0, 0, late], kv_half + n, mate).wait_send()

    @pl.loop(1, 8)
    def _(r):
        copy(ssq.at[0], ssq.at[0], ssq_n + r, mate).wait_send()

    @pl.when(core != zh)
    def _():
        back(0, 0).wait_send()

    pl.loop(1, 8)(lambda r: back(0, r).wait_send())
    pl.loop(0, 8)(lambda r: back(1, r).wait_send())


SEMS = 192


def body(
    query_rows, key_head_rows, value_head_rows, positions, residual, norm_gain, expert_ids,
    gate_fixed, w_gate, w_up, w_down,
):
    vmem = pl.BlockSpec(memory_space=pltpu.VMEM)
    hbm = pl.BlockSpec(memory_space=pl.ANY)
    return pl.pallas_call(
        kernel,
        out_shape=jax.ShapeDtypeStruct(residual.shape, BF16),
        in_specs=[vmem] * 8 + [hbm] * 3,
        out_specs=vmem,
        scratch_shapes=[
            pltpu.VMEM((2, 4, 4, 272, 128), BF16),
            pltpu.VMEM((8, 8, 128), F32),
            pltpu.VMEM((128, HALF), F32),
            pltpu.VMEM((128, EXPERTS * SLOT), BF16),
            pltpu.VMEM((2, 128, EXPERTS * SLOT), BF16),
            pltpu.VMEM((EXPERTS, SLOT, HALF), BF16),
            pltpu.VMEM((2, 8, SLOT, HALF), BF16),
            pltpu.VMEM((2, 2, 4, 2, ROWS, HALF), BF16),
            pltpu.VMEM(w_gate.shape[::-1], BF16),
            pltpu.VMEM(w_up.shape[::-1], BF16),
            pltpu.VMEM((2, w_down.shape[0], 2048), BF16),
            pltpu.VMEM((2, 2, ROWS, w_gate.shape[1]), F32),
            pltpu.VMEM((2, 2, ROWS, w_gate.shape[1]), F32),
            pltpu.VMEM((2, 2, 2, ROWS, w_gate.shape[1]), BF16),
            pltpu.VMEM((2, 4, 2, ROWS, HALF), BF16),
            pltpu.VMEM((2, QUARTER, HALF), BF16),
            pltpu.VMEM((7, ROWS, HALF), BF16),
            pltpu.VMEM((3, 2, ROWS, HALF), BF16),
            pltpu.VMEM((2, 8, SLOT, HALF), BF16),
            pltpu.VMEM((2, 8, SLOT, HALF), BF16),
            pltpu.SemaphoreType.DMA((SEMS,)),
            pltpu.SemaphoreType.DMA((SEMS,)),
            pltpu.SemaphoreType.DMA((3,)),
        ],
        compiler_params=pltpu.CompilerParams(
            collective_id=0, has_side_effects=True, vmem_limit_bytes=60 * 2**20
        ),
        cost_estimate=pl.CostEstimate(
            flops=14 * 10**9, bytes_accessed=12 * 10**6, transcendentals=3 * 10**6
        ),
    )(
        query_rows, key_head_rows, value_head_rows, expert_ids.T, gate_fixed.reshape(1, -1),
        positions.reshape(1, -1), residual, norm_gain.reshape(1, -1), w_gate.T, w_up.T, w_down,
    )


def solution(mesh):
    in_specs = (
        P("ctx", "head"),
        P("ctx", "head"),
        P("ctx", "head"),
        P("ctx"),
        P("ctx", "head"),
        P("head"),
        P("ctx", None),
        P("ctx"),
        P(None, ("ctx", "head")),
        P(None, ("ctx", "head")),
        P(("ctx", "head"), None),
    )
    out_specs = P("ctx", "head")
    return jax.shard_map(body, mesh=mesh, in_specs=in_specs, out_specs=out_specs, check_vma=False)
```

```python
import jax
import jax.numpy as jnp
from jax import lax
from jax.experimental import pallas as pl
from jax.experimental.pallas import tpu as pltpu
from jax.sharding import PartitionSpec as P

MESH = pl.DeviceIdType.MESH
HEAD_SIZE = 128
CAP = 36
PACK = 4 * CAP
EXPERTS = 8
ROWS = 8 * CAP
HALF = 512
QUARTER = ROWS // 2
SCALE = HEAD_SIZE ** (-0.5)
F32 = jnp.float32
BF16 = jnp.bfloat16


class Sems:
    def __init__(self, send, recv):
        self.send, self.recv, self.used = send, recv, 0

    def take(self, count=1):
        at = self.used
        self.used += count
        return at


def dot(a, b):
    return jnp.dot(a, b, preferred_element_type=F32)


def dot_t(a, b):
    return lax.dot_general(a, b, (((1,), (1,)), ((), ())), preferred_element_type=F32)


def fold(a):
    return jnp.concatenate([a[:, 128 * j : 128 * j + 128] for j in range(4)], axis=0)


def kernel(
    q_ref, k_ref, v_ref, ids_ref, gate_ref, pos_ref, resid_ref, gain_ref, wg_hbm, wu_hbm, wd_hbm,
    out_ref,
    kv, ssq, stream, pick, cw, turn, gbuf, d1, xb, wg, wu, wd, accg, accu, hid, yb, rq, rh, rf, r2s, r2,
    send, recv, local,
):
    c, h = lax.axis_index("ctx"), lax.axis_index("head")
    core, y, zl = lax.rem(c, 2), lax.rem(lax.div(c, 2), 4), lax.div(c, 8)
    yl, yh = lax.rem(y, 2), lax.div(y, 2)
    zh, x = lax.div(h, 4), lax.rem(h, 4)

    def at(zl_=zl, yh_=yh, yl_=yl, core_=core, zh_=zh, x_=x):
        return (zl_ * 8 + (yh_ * 2 + yl_) * 2 + core_, zh_ * 4 + x_)

    def kin(zl_=zl, yh_=yh, core_=core, zh_=zh):
        return at(zl_=zl_, yh_=yh_, yl_=lax.rem(yl + yh + yh_, 2), core_=core_, zh_=zh_)

    right, left = at(x_=lax.rem(x + 1, 4)), at(x_=lax.rem(x + 3, 4))
    across, mate = at(yl_=1 - yl), at(core_=1 - core)
    up, under = (
        at(yh_=lax.div(lax.rem(y + i, 4), 2), yl_=lax.rem(y + i, 2)) for i in (1, 3)
    )
    sems = Sems(send, recv)

    def copy(src, dst, n, device):
        return pltpu.make_async_remote_copy(
            src_ref=src, dst_ref=dst, send_sem=send.at[n], recv_sem=recv.at[n],
            device_id=device, device_id_type=MESH,
        )

    def arrive(dst, n):
        copy(dst, dst, n, mate).wait_recv()

    started = []

    def push(src, dst, n, device):
        copy(src, dst, n, device).start()
        started.append((src, n))

    loads = [
        pltpu.make_async_copy(wg_hbm, wg, local.at[0]),
        pltpu.make_async_copy(wu_hbm, wu, local.at[1]),
        pltpu.make_async_copy(
            wd_hbm.at[:, pl.ds(pl.multiple_of(core * 2048, 128), 2048)], wd.at[0], local.at[2]
        ),
    ]
    for load in loads:
        load.start()

    kv[0, 0, 0, 0:128, :] = k_ref[...]
    kv[0, 0, 0, 128:256, :] = v_ref[...]
    pos = pos_ref[...]
    pos_hi = lax.shift_right_logical(pos, 6).astype(F32)
    pos_lo = (pos & 63).astype(F32)
    row16 = lax.broadcasted_iota(jnp.int32, (16, 128), 0)
    kv[0, 0, 0, 256:272, :] = jnp.where(row16 == 0, pos_hi, pos_lo).astype(BF16)

    barrier = pltpu.get_barrier_semaphore()
    me32 = ((zh * 4 + zl) * 2 + yh) * 2 + core

    def greet(device):
        pl.semaphore_signal(barrier, inc=1, device_id=device, device_id_type=MESH)

    @pl.loop(1, 8)
    def _(r):
        greet((c, lax.rem(h + r, 8)))

    @pl.loop(1, 32)
    def _(r):
        j = lax.rem(me32 + r, 32)
        greet(
            kin(
                zl_=lax.rem(lax.div(j, 4), 4),
                yh_=lax.rem(lax.div(j, 2), 2),
                core_=lax.rem(j, 2),
                zh_=lax.div(j, 16),
            )
        )

    greet(up), greet(under)
    pl.semaphore_wait(barrier, 7 + 31 + 2)

    kv_n, kv_half, mate_n, wd_n = sems.take(16), sems.take(4), sems.take(16), sems.take()

    def kv_mate(dy, dz):
        n = mate_n + dy * 4 + dz
        copy(kv.at[0, dy, dz], kv.at[1, dy, dz], n, mate).start()

    def kv_round(dz):
        copy(kv.at[0, 0, dz], kv.at[0, 3, dz], kv_n + 12 + dz, up).start()
        copy(kv.at[0, 0, dz], kv.at[0, 1, dz], kv_n + 4 + dz, under).start()

    for dz in (3, 1, 2):
        copy(kv.at[0, 0, 0], kv.at[0, 0, dz], kv_n + dz, at(zl_=lax.rem(zl + 4 - dz, 4))).start()
    kv_round(0)
    kv_mate(0, 0)
    other = pl.multiple_of((1 - core) * 2048, 128)
    wd_move = copy(wd_hbm.at[:, pl.ds(other, 2048)], wd.at[1], wd_n, mate)
    wd_move.start()

    numbers = jnp.concatenate(
        [ids_ref[...].astype(F32), gate_ref[...].astype(F32), pos.astype(F32)] * 32, axis=0
    )
    numbers = jnp.transpose(numbers)
    ids0, ids1, gates, places = (numbers[:, i : i + 1] for i in range(4))

    q = fold(q_ref[...])
    q_pos = jnp.concatenate([places] * 4, axis=0)

    def attend(side, group, carry):
        top, total, acc = carry
        part = kv[side, group]
        keys = part[:, 0:128, :].reshape(512, 128)
        values = part[:, 128:256, :].reshape(512, 128)
        digits = part[:, 256:272, :].astype(F32)
        k_pos = jnp.concatenate(
            [digits[i, 0:1, :] * 64.0 + digits[i, 1:2, :] for i in range(4)], axis=1
        )
        scores = dot_t(q, keys)
        scores = jnp.where(k_pos <= q_pos, scores * SCALE, -1e30)
        new_top = jnp.maximum(top, jnp.max(scores, axis=1, keepdims=True))
        keep = jnp.exp(top - new_top)
        probs = jnp.exp(scores - new_top)
        total = total * keep + jnp.sum(probs, axis=1, keepdims=True)
        acc = acc * keep + dot(probs.astype(BF16), values)
        return new_top, total, acc

    early, late = pl.ds(0, 128), pl.ds(128, 144)

    def mate_side(step, carry):
        dy = step ^ lax.shift_right_logical(step, 1)
        for dz in range(4):
            arrive(kv.at[1, dy, dz], mate_n + dy * 4 + dz)
        return attend(1, dy, carry)

    carry = (jnp.full((512, 1), -1e30, F32), jnp.zeros((512, 1), F32), jnp.zeros((512, 128), F32))
    for dz in (1, 3, 2):
        arrive(kv.at[0, 0, dz], kv_n + dz)
        kv_round(dz)
        kv_mate(0, dz)
    carry = attend(0, 0, carry)
    for dz in (0, 1, 3, 2):
        arrive(kv.at[0, 3, dz], kv_n + 12 + dz)
        copy(kv.at[0, 3, dz, early], kv.at[0, 2, dz, early], kv_n + 8 + dz, up).start()
        kv_mate(3, dz)
        arrive(kv.at[0, 1, dz], kv_n + 4 + dz)
        copy(kv.at[0, 1, dz, late], kv.at[0, 2, dz, late], kv_half + dz, under).start()
        kv_mate(1, dz)
    carry = attend(0, 1, carry)
    carry = attend(0, 3, carry)
    for dz in (0, 1, 3, 2):
        arrive(kv.at[0, 2, dz, early], kv_n + 8 + dz)
        arrive(kv.at[0, 2, dz, late], kv_half + dz)
        kv_mate(2, dz)
    carry = attend(0, 2, carry)
    _, total, acc = lax.fori_loop(0, 4, mate_side, carry)
    att = (acc / total).astype(BF16).astype(F32)
    att = jnp.concatenate([att[128 * i : 128 * i + 128] for i in range(4)], axis=1)
    flow = resid_ref[...].astype(F32) + att
    stream[...] = flow

    own_sq = jnp.sum(flow * flow, axis=1, keepdims=True)
    ssq[0] = jnp.transpose(jnp.broadcast_to(own_sq, (128, 128)))[0:8, :]
    ssq_n = sems.take(8)

    @pl.loop(1, 8)
    def _(r):
        copy(ssq.at[0], ssq.at[r], ssq_n + r, (c, lax.rem(h + r, 8))).start()

    lane = lax.broadcasted_iota(jnp.int32, (128, 128), 1)
    below = lax.broadcasted_iota(jnp.int32, (128, 128), 0) > lane
    hit0, hit1 = lane.astype(F32) == ids0, lane.astype(F32) == ids1
    hits = jnp.where(hit0 | hit1, 1.0, 0.0).astype(BF16)
    ranks = dot(jnp.where(below, 1.0, 0.0).astype(BF16), hits)
    slot0 = ids0 * PACK + jnp.sum(jnp.where(hit0, ranks, 0.0), axis=1, keepdims=True)
    slot1 = ids1 * PACK + jnp.sum(jnp.where(hit1, ranks, 0.0), axis=1, keepdims=True)
    row0, row1 = (
        jnp.transpose(jnp.broadcast_to(slot, (128, 128)))[0:1, :] for slot in (slot0, slot1)
    )
    slots = lax.broadcasted_iota(jnp.int32, (EXPERTS * PACK, 128), 0).astype(F32)
    for j in range(4):
        hit = (slots == row0 + CAP * j) | (slots == row1 + CAP * j)
        pick[:, 128 * j : 128 * j + 128] = jnp.where(hit, 1.0, 0.0).astype(BF16)

    @pl.loop(1, 8)
    def _(r):
        arrive(ssq.at[r], ssq_n + r)

    all_sq = jnp.sum(ssq[...], axis=0)
    all_sq = jnp.transpose(jnp.concatenate([all_sq] * 16, axis=0))[:, 0:1]
    normed = flow * lax.rsqrt(all_sq / 4096.0 + 1e-05) * gain_ref[...].astype(F32)
    rows = dot(pick[...], fold(normed.astype(BF16)))
    gbuf[...] = rows.astype(BF16).reshape(EXPERTS, PACK, 128)

    d1_n = sems.take(16)
    me8 = zl * 2 + yh

    def dispatch(i, r):
        e = lax.rem(me8 + r, 8)
        device = kin(zl_=lax.div(e, 2), yh_=lax.rem(e, 2), zh_=zh if i == 0 else 1 - zh)
        copy(gbuf.at[e], d1.at[i, me8], d1_n + 8 * i + r, device).start()

    pl.loop(1, 8)(lambda r: dispatch(0, r))
    pl.loop(0, 8)(lambda r: dispatch(1, r))
    d1[0, me8] = gbuf[me8]

    def dispatched(i, r):
        arrive(d1.at[i, lax.rem(me8 + 8 - r, 8)], d1_n + 8 * i + r)

    here = lax.broadcasted_iota(jnp.int32, (4 * PACK, 1), 0)
    outer = sum([jnp.where(here >= PACK * i, 1, 0) for i in range(1, 4)])
    inner = sum([jnp.where(here - outer * PACK >= CAP * i, 1, 0) for i in range(1, 4)])
    there = lax.broadcasted_iota(jnp.int32, (4 * PACK, 4 * PACK), 1)
    turn[...] = jnp.where(there == here + (inner - outer) * (PACK - CAP), 1.0, 0.0).astype(BF16)

    def compacted(i):
        for g in range(2):
            turned = dot(turn[...], d1[i, 4 * g : 4 * g + 4].reshape(4 * PACK, 128)).astype(BF16)
            for j in range(4):
                xb[0, 0, 0, i, PACK * g : PACK * g + PACK, 128 * j : 128 * j + 128] = turned[
                    PACK * j : PACK * j + PACK
                ]

    got = {}

    def relay(src, way, rows_of=None):
        side, dy, dx, i = src
        device, to = {
            "r": (right, (0, dy, (dx + 3) % 4, i)),
            "l": (left, (0, dy, (dx + 1) % 4, i)),
            "y": (across, (0, 1 - dy, dx, i)),
            "m": (mate, (1, dy, dx, i)),
        }[way]
        n = sems.take()
        part, there = xb.at[src], xb.at[to]
        if rows_of is not None:
            part = part.at[pl.ds(rows_of * QUARTER, QUARTER)]
            there = there.at[pl.ds(rows_of * QUARTER, QUARTER)]
        push(part, there, n, device)
        got[(*to, rows_of)] = (there, n)

    def landed(slot, rows_of=None):
        there, n = got[(*slot, rows_of)]
        arrive(there, n)

    def multiply(side, dy, dx):
        xs = lax.rem(x + dx, 4)
        low = pl.ds(pl.multiple_of((zh * 4 + xs) * HALF, HALF), HALF)
        high = pl.ds(pl.multiple_of(((1 - zh) * 4 + xs) * HALF, HALF), HALF)
        a, b = xb[side, dy, dx, 0], xb[side, dy, dx, 1]
        accg[side, dy] += dot_t(a, wg[:, low]) + dot_t(b, wg[:, high])
        accu[side, dy] += dot_t(a, wu[:, low]) + dot_t(b, wu[:, high])

    hid_n = {}

    def hide(side, dy):
        g = accg[side, dy]
        hid[0, side, dy] = (g / (1.0 + jnp.exp(-g)) * accu[side, dy]).astype(BF16)
        n = hid_n[1 - side, dy] = sems.take()
        push(hid.at[0, side, dy], hid.at[1, 1 - side, dy], n, mate)

    def shared(dy):
        for side in range(2):
            arrive(hid.at[1, side, dy], hid_n[side, dy])

    own = [(0, 0, 0, 0), (0, 0, 0, 1)]
    pl.loop(1, 8)(lambda r: dispatched(0, r))
    compacted(0)
    relay(own[0], "r"), relay(own[0], "l"), relay(own[0], "y"), relay(own[0], "m")
    for load in loads[:2]:
        load.wait()
    accg[...] = jnp.zeros_like(accg)
    accu[...] = jnp.zeros_like(accu)
    pl.loop(0, 8)(lambda r: dispatched(1, r))
    compacted(1)
    relay(own[1], "l"), relay(own[1], "r"), relay(own[1], "y"), relay(own[1], "m")
    lanes = lax.broadcasted_iota(jnp.int32, (128, EXPERTS * PACK), 1).astype(F32)
    first = gates / 65536.0
    for j in range(4):
        weights = jnp.where(lanes == slot0 + CAP * j, first, 0.0)
        weights += jnp.where(lanes == slot1 + CAP * j, 1.0 - first, 0.0)
        coarse = weights.astype(BF16)
        cw[0, 128 * j : 128 * j + 128] = coarse
        cw[1, 128 * j : 128 * j + 128] = (weights - coarse.astype(F32)).astype(BF16)
    landed((0, 0, 3, 0)), relay((0, 0, 3, 0), "r")
    landed((0, 1, 0, 0)), relay((0, 1, 0, 0), "r"), relay((0, 1, 0, 0), "l")
    multiply(0, 0, 0)
    landed((0, 0, 1, 1)), relay((0, 0, 1, 1), "l"), relay((0, 0, 1, 1), "y")
    landed((0, 0, 3, 1)), relay((0, 0, 3, 1), "y")
    landed((0, 0, 1, 0)), landed((0, 1, 0, 1))
    for slot in ((0, 3), (0, 1), (1, 0)):
        for i in range(2):
            relay((0, *slot, i), "m")
    landed((1, 0, 0, 0)), landed((1, 0, 0, 1))
    multiply(1, 0, 0)
    multiply(0, 0, 3)
    landed((0, 0, 2, 1)), relay((0, 0, 2, 1), "y"), relay((0, 0, 2, 1), "m")
    landed((0, 1, 3, 0)), relay((0, 1, 3, 0), "r", 0), relay((0, 1, 3, 0), "m")
    landed((0, 1, 1, 0)), relay((0, 1, 1, 0), "l", 1), relay((0, 1, 1, 0), "m")
    landed((0, 0, 2, 0)), relay((0, 0, 2, 0), "m")
    multiply(0, 0, 1)
    multiply(0, 1, 0)
    multiply(0, 0, 2)
    for slot in ((0, 3), (0, 1), (1, 0)):
        landed((1, *slot, 0)), landed((1, *slot, 1))
        multiply(1, *slot)
    landed((0, 1, 1, 1)), relay((0, 1, 1, 1), "m")
    landed((0, 1, 3, 1)), relay((0, 1, 3, 1), "m")
    multiply(0, 1, 1)
    multiply(0, 1, 3)
    landed((1, 0, 2, 0)), landed((1, 0, 2, 1))
    multiply(1, 0, 2)
    hide(0, 0), hide(1, 0)
    landed((0, 1, 2, 0), 0), landed((0, 1, 2, 0), 1), relay((0, 1, 2, 0), "m")
    landed((0, 1, 2, 1)), relay((0, 1, 2, 1), "m")
    for slot in ((1, 1), (1, 3)):
        landed((1, *slot, 0)), landed((1, *slot, 1))
        multiply(1, *slot)
    multiply(0, 1, 2)
    landed((1, 1, 2, 0)), landed((1, 1, 2, 1))
    multiply(1, 1, 2)

    hide(0, 1), hide(1, 1)

    def down(dy, dx):
        columns = pl.ds(pl.multiple_of(lax.rem(x + dx, 4) * HALF, HALF), HALF)
        for i in range(2):
            yb[dy, dx, i] = (
                dot(hid[0, i, dy], wd[0, :, columns]) + dot(hid[1, i, dy], wd[1, :, columns])
            ).astype(BF16)

    def add(into, *terms):
        value = into[...].astype(F32)
        for ref, _ in terms:
            value += ref[...].astype(F32)
        into[...] = value.astype(BF16)

    def give(src, dst, device):
        n = sems.take()
        push(src, dst, n, device)
        return dst, n

    def wait_all(*terms):
        for ref, n in terms:
            arrive(ref, n)

    loads[2].wait()
    wd_move.wait()
    shared(0)
    down(0, 2)
    from_r_2 = give(yb.at[0, 2, 0], rh.at[1], left)
    shared(1)
    down(1, 2)
    from_y2 = give(yb.at[1, 2, 1], rh.at[0], across)
    from_r_q = give(yb.at[1, 2, 0, pl.ds(0, QUARTER)], rq.at[0], left)
    from_l_q = give(yb.at[1, 2, 0, pl.ds(QUARTER, QUARTER)], rq.at[1], right)
    down(1, 3)
    from_y_3 = give(yb.at[1, 3, 1], rh.at[2], across)
    down(1, 1)
    from_y_1 = give(yb.at[1, 1, 1], rh.at[3], across)
    wait_all(from_y2, from_r_q, from_l_q)
    add(yb.at[0, 2, 1], from_y2)
    from_l_2 = give(yb.at[0, 2, 1], rh.at[4], right)
    add(yb.at[1, 3, 0, pl.ds(0, QUARTER)], from_r_q)
    from_r_3 = give(yb.at[1, 3, 0], rh.at[5], left)
    add(yb.at[1, 1, 0, pl.ds(QUARTER, QUARTER)], from_l_q)
    from_l_1 = give(yb.at[1, 1, 0], rh.at[6], right)
    down(0, 1)
    last_l = [give(yb.at[0, 1, 0], rf.at[0, 0], right), None]
    down(1, 0)
    last_y = [None, give(yb.at[1, 0, 1], rf.at[1, 1], across)]
    down(0, 3)
    wait_all(from_r_2)
    add(yb.at[0, 3, 0], from_r_2)
    last_r = [give(yb.at[0, 3, 0], rf.at[2, 0], left), None]
    wait_all(from_y_3)
    add(yb.at[0, 3, 1], from_y_3)
    last_r[1] = give(yb.at[0, 3, 1], rf.at[2, 1], left)
    wait_all(from_y_1, from_l_2)
    add(yb.at[0, 1, 1], from_y_1, from_l_2)
    last_l[1] = give(yb.at[0, 1, 1], rf.at[0, 1], right)
    wait_all(from_r_3, from_l_1)
    add(yb.at[1, 0, 0], from_r_3, from_l_1)
    last_y[0] = give(yb.at[1, 0, 0], rf.at[1, 0], across)
    down(0, 0)

    r2_n = sems.take(16)
    r2_s = sems.take(16)

    far = lax.rem(zh + core, 2)

    def back(i, r):
        s = lax.rem(me8 + r, 8)
        device = kin(
            zl_=lax.div(s, 2), yh_=lax.rem(s, 2), core_=core if i == 0 else 1 - core, zh_=core
        )
        return pltpu.make_async_remote_copy(
            src_ref=r2s.at[i, s], dst_ref=r2.at[far, me8],
            send_sem=send.at[r2_s + 8 * i + r], recv_sem=recv.at[r2_n + far * 8 + me8],
            device_id=device, device_id_type=MESH,
        )

    for i in range(2):
        wait_all(last_l[i], last_r[i], last_y[i])
        value = (
            yb[0, 0, i].astype(F32)
            + rf[0, i].astype(F32)
            + rf[1, i].astype(F32)
            + rf[2, i].astype(F32)
        ).astype(BF16)
        for g in range(2):
            turned = dot(turn[...], fold(value[PACK * g : PACK * g + PACK]))
            r2s[i, 4 * g : 4 * g + 4] = turned.astype(BF16).reshape(4, PACK, 128)
        if i == 0:

            @pl.when(core == zh)
            def _():
                r2[0, me8] = r2s[0, me8]

            @pl.when(core != zh)
            def _():
                back(0, 0).start()

            pl.loop(1, 8)(lambda r: back(0, r).start())
        else:
            pl.loop(0, 8)(lambda r: back(1, r).start())

    def weighted(i):
        back_rows = r2[i].reshape(EXPERTS * PACK, 128)
        mixed = dot(cw[0], back_rows) + dot(cw[1], back_rows)
        return jnp.concatenate([mixed[128 * j : 128 * j + 128] for j in range(4)], axis=1)

    def returned(i, r):
        e = lax.rem(me8 + r, 8)
        arrive(r2.at[i, e], r2_n + 8 * i + e)

    pl.loop(1, 8)(lambda r: returned(0, r))

    @pl.when(core != zh)
    def _():
        returned(0, 0)

    mix = stream[...] + weighted(0)
    pl.loop(0, 8)(lambda r: returned(1, r))
    mix += weighted(1)
    out_ref[...] = mix.astype(BF16)

    for src, n in started:
        copy(src, src, n, mate).wait_send()

    @pl.loop(1, 16)
    def _(r):
        copy(gbuf.at[0], gbuf.at[0], d1_n + r, mate).wait_send()

    @pl.loop(0, 16)
    def _(r):
        copy(kv.at[0, 0, 0], kv.at[0, 0, 0], mate_n + r, mate).wait_send()

    for n in (*range(1, 8), *range(12, 16)):
        copy(kv.at[0, 0, 0], kv.at[0, 0, 0], kv_n + n, mate).wait_send()
    for n in range(4):
        copy(kv.at[0, 0, 0, early], kv.at[0, 0, 0, early], kv_n + 8 + n, mate).wait_send()
        copy(kv.at[0, 0, 0, late], kv.at[0, 0, 0, late], kv_half + n, mate).wait_send()

    @pl.loop(1, 8)
    def _(r):
        copy(ssq.at[0], ssq.at[0], ssq_n + r, mate).wait_send()

    @pl.when(core != zh)
    def _():
        back(0, 0).wait_send()

    pl.loop(1, 8)(lambda r: back(0, r).wait_send())
    pl.loop(0, 8)(lambda r: back(1, r).wait_send())


SEMS = 192


def body(
    query_rows, key_head_rows, value_head_rows, positions, residual, norm_gain, expert_ids,
    gate_fixed, w_gate, w_up, w_down,
):
    vmem = pl.BlockSpec(memory_space=pltpu.VMEM)
    hbm = pl.BlockSpec(memory_space=pl.ANY)
    return pl.pallas_call(
        kernel,
        out_shape=jax.ShapeDtypeStruct(residual.shape, BF16),
        in_specs=[vmem] * 8 + [hbm] * 3,
        out_specs=vmem,
        scratch_shapes=[
            pltpu.VMEM((2, 4, 4, 272, 128), BF16),
            pltpu.VMEM((8, 8, 128), F32),
            pltpu.VMEM((128, HALF), F32),
            pltpu.VMEM((EXPERTS * PACK, HALF), BF16),
            pltpu.VMEM((2, HALF, EXPERTS * PACK), BF16),
            pltpu.VMEM((4 * PACK, 4 * PACK), BF16),
            pltpu.VMEM((EXPERTS, PACK, 128), BF16),
            pltpu.VMEM((2, 8, PACK, 128), BF16),
            pltpu.VMEM((2, 2, 4, 2, ROWS, HALF), BF16),
            pltpu.VMEM(w_gate.shape[::-1], BF16),
            pltpu.VMEM(w_up.shape[::-1], BF16),
            pltpu.VMEM((2, w_down.shape[0], 2048), BF16),
            pltpu.VMEM((2, 2, ROWS, w_gate.shape[1]), F32),
            pltpu.VMEM((2, 2, ROWS, w_gate.shape[1]), F32),
            pltpu.VMEM((2, 2, 2, ROWS, w_gate.shape[1]), BF16),
            pltpu.VMEM((2, 4, 2, ROWS, HALF), BF16),
            pltpu.VMEM((2, QUARTER, HALF), BF16),
            pltpu.VMEM((7, ROWS, HALF), BF16),
            pltpu.VMEM((3, 2, ROWS, HALF), BF16),
            pltpu.VMEM((2, 8, PACK, 128), BF16),
            pltpu.VMEM((2, 8, PACK, 128), BF16),
            pltpu.SemaphoreType.DMA((SEMS,)),
            pltpu.SemaphoreType.DMA((SEMS,)),
            pltpu.SemaphoreType.DMA((3,)),
        ],
        compiler_params=pltpu.CompilerParams(
            collective_id=0, has_side_effects=True, vmem_limit_bytes=60 * 2**20
        ),
        cost_estimate=pl.CostEstimate(
            flops=14 * 10**9, bytes_accessed=12 * 10**6, transcendentals=3 * 10**6
        ),
    )(
        query_rows, key_head_rows, value_head_rows, expert_ids.T, gate_fixed.reshape(1, -1),
        positions.reshape(1, -1), residual, norm_gain.reshape(1, -1), w_gate.T, w_up.T, w_down,
    )


def solution(mesh):
    in_specs = (
        P("ctx", "head"),
        P("ctx", "head"),
        P("ctx", "head"),
        P("ctx"),
        P("ctx", "head"),
        P("head"),
        P("ctx", None),
        P("ctx"),
        P(None, ("ctx", "head")),
        P(None, ("ctx", "head")),
        P(("ctx", "head"), None),
    )
    out_specs = P("ctx", "head")
    return jax.shard_map(body, mesh=mesh, in_specs=in_specs, out_specs=out_specs, check_vma=False)
```

```python
import jax
import jax.numpy as jnp
from jax import lax
from jax.experimental import pallas as pl
from jax.experimental.pallas import tpu as pltpu
from jax.sharding import PartitionSpec as P

MESH = pl.DeviceIdType.MESH
HEAD_SIZE = 128
CAP = 36
PACK = 4 * CAP
EXPERTS = 8
ROWS = 8 * CAP
HALF = 512
QUARTER = ROWS // 2
SCALE = HEAD_SIZE ** (-0.5)
F32 = jnp.float32
BF16 = jnp.bfloat16


class Sems:
    def __init__(self, send, recv):
        self.send, self.recv, self.used = send, recv, 0

    def take(self, count=1):
        at = self.used
        self.used += count
        return at


def dot(a, b):
    return jnp.dot(a, b, preferred_element_type=F32)


def dot_t(a, b):
    return lax.dot_general(a, b, (((1,), (1,)), ((), ())), preferred_element_type=F32)


def fold(a):
    return jnp.concatenate([a[:, 128 * j : 128 * j + 128] for j in range(4)], axis=0)


def kernel(
    q_ref, k_ref, v_ref, ids_ref, gate_ref, pos_ref, resid_ref, gain_ref, wg_hbm, wu_hbm, wd_hbm,
    out_ref,
    kv, ssq, stream, pick, cw, turn, gbuf, d1, xb, wg, wu, wd, accg, accu, hid, yb, rq, rh, rf, r2s, r2,
    send, recv, local,
):
    c, h = lax.axis_index("ctx"), lax.axis_index("head")
    core, y, zl = lax.rem(c, 2), lax.rem(lax.div(c, 2), 4), lax.div(c, 8)
    yl, yh = lax.rem(y, 2), lax.div(y, 2)
    zh, x = lax.div(h, 4), lax.rem(h, 4)

    def at(zl_=zl, yh_=yh, yl_=yl, core_=core, zh_=zh, x_=x):
        return (zl_ * 8 + (yh_ * 2 + yl_) * 2 + core_, zh_ * 4 + x_)

    def kin(zl_=zl, yh_=yh, core_=core, zh_=zh):
        return at(zl_=zl_, yh_=yh_, yl_=lax.rem(yl + yh + yh_, 2), core_=core_, zh_=zh_)

    right, left = at(x_=lax.rem(x + 1, 4)), at(x_=lax.rem(x + 3, 4))
    across, mate = at(yl_=1 - yl), at(core_=1 - core)
    up, under = (
        at(yh_=lax.div(lax.rem(y + i, 4), 2), yl_=lax.rem(y + i, 2)) for i in (1, 3)
    )
    sems = Sems(send, recv)

    def copy(src, dst, n, device):
        return pltpu.make_async_remote_copy(
            src_ref=src, dst_ref=dst, send_sem=send.at[n], recv_sem=recv.at[n],
            device_id=device, device_id_type=MESH,
        )

    def arrive(dst, n):
        copy(dst, dst, n, mate).wait_recv()

    started = []

    def push(src, dst, n, device):
        copy(src, dst, n, device).start()
        started.append((src, n))

    loads = [
        pltpu.make_async_copy(wg_hbm, wg, local.at[0]),
        pltpu.make_async_copy(wu_hbm, wu, local.at[1]),
        pltpu.make_async_copy(
            wd_hbm.at[:, pl.ds(pl.multiple_of(core * 2048, 128), 2048)], wd.at[0], local.at[2]
        ),
    ]
    for load in loads:
        load.start()

    kv[0, 0, 0, 0:128, :] = k_ref[...]
    kv[0, 0, 0, 128:256, :] = v_ref[...]
    pos = pos_ref[...]
    pos_hi = lax.shift_right_logical(pos, 6).astype(F32)
    pos_lo = (pos & 63).astype(F32)
    row16 = lax.broadcasted_iota(jnp.int32, (16, 128), 0)
    kv[0, 0, 0, 256:272, :] = jnp.where(row16 == 0, pos_hi, pos_lo).astype(BF16)

    barrier = pltpu.get_barrier_semaphore()
    me32 = ((zh * 4 + zl) * 2 + yh) * 2 + core

    def greet(device):
        pl.semaphore_signal(barrier, inc=1, device_id=device, device_id_type=MESH)

    @pl.loop(1, 8)
    def _(r):
        greet((c, lax.rem(h + r, 8)))

    @pl.loop(1, 32)
    def _(r):
        j = lax.rem(me32 + r, 32)
        greet(
            kin(
                zl_=lax.rem(lax.div(j, 4), 4),
                yh_=lax.rem(lax.div(j, 2), 2),
                core_=lax.rem(j, 2),
                zh_=lax.div(j, 16),
            )
        )

    greet(up), greet(under)
    pl.semaphore_wait(barrier, 7 + 31 + 2)

    kv_n, kv_half, mate_n, wd_n = sems.take(16), sems.take(4), sems.take(16), sems.take()

    def kv_mate(dy, dz):
        n = mate_n + dy * 4 + dz
        copy(kv.at[0, dy, dz], kv.at[1, dy, dz], n, mate).start()

    def kv_round(dz):
        copy(kv.at[0, 0, dz], kv.at[0, 3, dz], kv_n + 12 + dz, up).start()
        copy(kv.at[0, 0, dz], kv.at[0, 1, dz], kv_n + 4 + dz, under).start()

    for dz in (3, 1, 2):
        copy(kv.at[0, 0, 0], kv.at[0, 0, dz], kv_n + dz, at(zl_=lax.rem(zl + 4 - dz, 4))).start()
    kv_round(0)
    kv_mate(0, 0)
    other = pl.multiple_of((1 - core) * 2048, 128)
    wd_move = copy(wd_hbm.at[:, pl.ds(other, 2048)], wd.at[1], wd_n, mate)
    wd_move.start()

    numbers = jnp.concatenate(
        [ids_ref[...].astype(F32), gate_ref[...].astype(F32), pos.astype(F32)] * 32, axis=0
    )
    numbers = jnp.transpose(numbers)
    ids0, ids1, gates, places = (numbers[:, i : i + 1] for i in range(4))

    q = fold(q_ref[...])
    q_pos = jnp.concatenate([places] * 4, axis=0)

    def attend(side, group, carry):
        top, total, acc = carry
        part = kv[side, group]
        keys = part[:, 0:128, :].reshape(512, 128)
        values = part[:, 128:256, :].reshape(512, 128)
        digits = part[:, 256:272, :].astype(F32)
        k_pos = jnp.concatenate(
            [digits[i, 0:1, :] * 64.0 + digits[i, 1:2, :] for i in range(4)], axis=1
        )
        scores = dot_t(q, keys)
        scores = jnp.where(k_pos <= q_pos, scores * SCALE, -1e30)
        new_top = jnp.maximum(top, jnp.max(scores, axis=1, keepdims=True))
        keep = jnp.exp(top - new_top)
        probs = jnp.exp(scores - new_top)
        total = total * keep + jnp.sum(probs, axis=1, keepdims=True)
        acc = acc * keep + dot(probs.astype(BF16), values)
        return new_top, total, acc

    early, late = pl.ds(0, 128), pl.ds(128, 144)

    def mate_side(step, carry):
        dy = step ^ lax.shift_right_logical(step, 1)
        for dz in range(4):
            arrive(kv.at[1, dy, dz], mate_n + dy * 4 + dz)
        return attend(1, dy, carry)

    carry = (jnp.full((512, 1), -1e30, F32), jnp.zeros((512, 1), F32), jnp.zeros((512, 128), F32))
    for dz in (1, 3, 2):
        arrive(kv.at[0, 0, dz], kv_n + dz)
        kv_round(dz)
        kv_mate(0, dz)
    carry = attend(0, 0, carry)
    for dz in (0, 1, 3, 2):
        arrive(kv.at[0, 3, dz], kv_n + 12 + dz)
        copy(kv.at[0, 3, dz, early], kv.at[0, 2, dz, early], kv_n + 8 + dz, up).start()
        kv_mate(3, dz)
        arrive(kv.at[0, 1, dz], kv_n + 4 + dz)
        copy(kv.at[0, 1, dz, late], kv.at[0, 2, dz, late], kv_half + dz, under).start()
        kv_mate(1, dz)
    carry = attend(0, 1, carry)
    carry = attend(0, 3, carry)
    for dz in (0, 1, 3, 2):
        arrive(kv.at[0, 2, dz, early], kv_n + 8 + dz)
        arrive(kv.at[0, 2, dz, late], kv_half + dz)
        kv_mate(2, dz)
    carry = attend(0, 2, carry)
    _, total, acc = lax.fori_loop(0, 4, mate_side, carry)
    att = (acc / total).astype(BF16).astype(F32)
    att = jnp.concatenate([att[128 * i : 128 * i + 128] for i in range(4)], axis=1)
    flow = resid_ref[...].astype(F32) + att
    stream[...] = flow

    own_sq = jnp.sum(flow * flow, axis=1, keepdims=True)
    ssq[0] = jnp.transpose(jnp.broadcast_to(own_sq, (128, 128)))[0:8, :]
    ssq_n = sems.take(8)

    @pl.loop(1, 8)
    def _(r):
        copy(ssq.at[0], ssq.at[r], ssq_n + r, (c, lax.rem(h + r, 8))).start()

    lane = lax.broadcasted_iota(jnp.int32, (128, 128), 1)
    below = lax.broadcasted_iota(jnp.int32, (128, 128), 0) > lane
    hit0, hit1 = lane.astype(F32) == ids0, lane.astype(F32) == ids1
    hits = jnp.where(hit0 | hit1, 1.0, 0.0).astype(BF16)
    ranks = dot(jnp.where(below, 1.0, 0.0).astype(BF16), hits)
    slot0 = ids0 * PACK + jnp.sum(jnp.where(hit0, ranks, 0.0), axis=1, keepdims=True)
    slot1 = ids1 * PACK + jnp.sum(jnp.where(hit1, ranks, 0.0), axis=1, keepdims=True)
    row0, row1 = (
        jnp.transpose(jnp.broadcast_to(slot, (128, 128)))[0:1, :] for slot in (slot0, slot1)
    )
    slots = lax.broadcasted_iota(jnp.int32, (EXPERTS * PACK, 128), 0).astype(F32)
    for j in range(4):
        hit = (slots == row0 + CAP * j) | (slots == row1 + CAP * j)
        pick[:, 128 * j : 128 * j + 128] = jnp.where(hit, 1.0, 0.0).astype(BF16)

    @pl.loop(1, 8)
    def _(r):
        arrive(ssq.at[r], ssq_n + r)

    all_sq = jnp.sum(ssq[...], axis=0)
    all_sq = jnp.transpose(jnp.concatenate([all_sq] * 16, axis=0))[:, 0:1]
    gains = gain_ref[...].astype(F32)
    gains = jnp.concatenate([gains[j : j + 1] for j in range(4)], axis=1)
    normed = flow * lax.rsqrt(all_sq / 4096.0 + 1e-05) * gains
    rows = dot(pick[...], fold(normed.astype(BF16)))
    gbuf[...] = rows.astype(BF16).reshape(EXPERTS, PACK, 128)

    d1_n = sems.take(16)
    me8 = zl * 2 + yh

    def dispatch(i, r):
        e = lax.rem(me8 + r, 8)
        device = kin(zl_=lax.div(e, 2), yh_=lax.rem(e, 2), zh_=zh if i == 0 else 1 - zh)
        copy(gbuf.at[e], d1.at[i, me8], d1_n + 8 * i + r, device).start()

    pl.loop(1, 8)(lambda r: dispatch(0, r))
    pl.loop(0, 8)(lambda r: dispatch(1, r))
    d1[0, me8] = gbuf[me8]

    def dispatched(i, r):
        arrive(d1.at[i, lax.rem(me8 + 8 - r, 8)], d1_n + 8 * i + r)

    here = lax.broadcasted_iota(jnp.int32, (4 * PACK, 1), 0)
    outer = sum([jnp.where(here >= PACK * i, 1, 0) for i in range(1, 4)])
    inner = sum([jnp.where(here - outer * PACK >= CAP * i, 1, 0) for i in range(1, 4)])
    there = lax.broadcasted_iota(jnp.int32, (4 * PACK, 4 * PACK), 1)
    turn[...] = jnp.where(there == here + (inner - outer) * (PACK - CAP), 1.0, 0.0).astype(BF16)

    def compacted(i):
        for g in range(2):
            turned = dot(turn[...], d1[i, 4 * g : 4 * g + 4].reshape(4 * PACK, 128)).astype(BF16)
            for j in range(4):
                xb[0, 0, 0, i, PACK * g : PACK * g + PACK, 128 * j : 128 * j + 128] = turned[
                    PACK * j : PACK * j + PACK
                ]

    got = {}

    def relay(src, way, rows_of=None):
        side, dy, dx, i = src
        device, to = {
            "r": (right, (0, dy, (dx + 3) % 4, i)),
            "l": (left, (0, dy, (dx + 1) % 4, i)),
            "y": (across, (0, 1 - dy, dx, i)),
            "m": (mate, (1, dy, dx, i)),
        }[way]
        n = sems.take()
        part, there = xb.at[src], xb.at[to]
        if rows_of is not None:
            part = part.at[pl.ds(rows_of * QUARTER, QUARTER)]
            there = there.at[pl.ds(rows_of * QUARTER, QUARTER)]
        push(part, there, n, device)
        got[(*to, rows_of)] = (there, n)

    def landed(slot, rows_of=None):
        there, n = got[(*slot, rows_of)]
        arrive(there, n)

    def multiply(side, dy, dx):
        xs = lax.rem(x + dx, 4)
        low = pl.ds(pl.multiple_of((zh * 4 + xs) * HALF, HALF), HALF)
        high = pl.ds(pl.multiple_of(((1 - zh) * 4 + xs) * HALF, HALF), HALF)
        a, b = xb[side, dy, dx, 0], xb[side, dy, dx, 1]
        accg[side, dy] += dot_t(a, wg[:, low]) + dot_t(b, wg[:, high])
        accu[side, dy] += dot_t(a, wu[:, low]) + dot_t(b, wu[:, high])

    hid_n = {}

    def hide(side, dy):
        g = accg[side, dy]
        hid[0, side, dy] = (g / (1.0 + jnp.exp(-g)) * accu[side, dy]).astype(BF16)
        n = hid_n[1 - side, dy] = sems.take()
        push(hid.at[0, side, dy], hid.at[1, 1 - side, dy], n, mate)

    def shared(dy):
        for side in range(2):
            arrive(hid.at[1, side, dy], hid_n[side, dy])

    own = [(0, 0, 0, 0), (0, 0, 0, 1)]
    pl.loop(1, 8)(lambda r: dispatched(0, r))
    compacted(0)
    relay(own[0], "r"), relay(own[0], "l"), relay(own[0], "y"), relay(own[0], "m")
    for load in loads[:2]:
        load.wait()
    accg[...] = jnp.zeros_like(accg)
    accu[...] = jnp.zeros_like(accu)
    pl.loop(0, 8)(lambda r: dispatched(1, r))
    compacted(1)
    relay(own[1], "l"), relay(own[1], "r"), relay(own[1], "y"), relay(own[1], "m")
    lanes = lax.broadcasted_iota(jnp.int32, (128, EXPERTS * PACK), 1).astype(F32)
    first = gates / 65536.0
    for j in range(4):
        weights = jnp.where(lanes == slot0 + CAP * j, first, 0.0)
        weights += jnp.where(lanes == slot1 + CAP * j, 1.0 - first, 0.0)
        coarse = weights.astype(BF16)
        cw[0, 128 * j : 128 * j + 128] = coarse
        cw[1, 128 * j : 128 * j + 128] = (weights - coarse.astype(F32)).astype(BF16)
    landed((0, 0, 3, 0)), relay((0, 0, 3, 0), "r")
    landed((0, 1, 0, 0)), relay((0, 1, 0, 0), "r"), relay((0, 1, 0, 0), "l")
    multiply(0, 0, 0)
    landed((0, 0, 1, 1)), relay((0, 0, 1, 1), "l"), relay((0, 0, 1, 1), "y")
    landed((0, 0, 3, 1)), relay((0, 0, 3, 1), "y")
    landed((0, 0, 1, 0)), landed((0, 1, 0, 1))
    for slot in ((0, 3), (0, 1), (1, 0)):
        for i in range(2):
            relay((0, *slot, i), "m")
    landed((1, 0, 0, 0)), landed((1, 0, 0, 1))
    multiply(1, 0, 0)
    multiply(0, 0, 3)
    landed((0, 0, 2, 1)), relay((0, 0, 2, 1), "y"), relay((0, 0, 2, 1), "m")
    landed((0, 1, 3, 0)), relay((0, 1, 3, 0), "r", 0), relay((0, 1, 3, 0), "m")
    landed((0, 1, 1, 0)), relay((0, 1, 1, 0), "l", 1), relay((0, 1, 1, 0), "m")
    landed((0, 0, 2, 0)), relay((0, 0, 2, 0), "m")
    multiply(0, 0, 1)
    multiply(0, 1, 0)
    multiply(0, 0, 2)
    for slot in ((0, 3), (0, 1), (1, 0)):
        landed((1, *slot, 0)), landed((1, *slot, 1))
        multiply(1, *slot)
    landed((0, 1, 1, 1)), relay((0, 1, 1, 1), "m")
    landed((0, 1, 3, 1)), relay((0, 1, 3, 1), "m")
    multiply(0, 1, 1)
    multiply(0, 1, 3)
    landed((1, 0, 2, 0)), landed((1, 0, 2, 1))
    multiply(1, 0, 2)
    hide(0, 0), hide(1, 0)
    landed((0, 1, 2, 0), 0), landed((0, 1, 2, 0), 1), relay((0, 1, 2, 0), "m")
    landed((0, 1, 2, 1)), relay((0, 1, 2, 1), "m")
    for slot in ((1, 1), (1, 3)):
        landed((1, *slot, 0)), landed((1, *slot, 1))
        multiply(1, *slot)
    multiply(0, 1, 2)
    landed((1, 1, 2, 0)), landed((1, 1, 2, 1))
    multiply(1, 1, 2)

    hide(0, 1), hide(1, 1)

    def down(dy, dx):
        columns = pl.ds(pl.multiple_of(lax.rem(x + dx, 4) * HALF, HALF), HALF)
        for i in range(2):
            yb[dy, dx, i] = (
                dot(hid[0, i, dy], wd[0, :, columns]) + dot(hid[1, i, dy], wd[1, :, columns])
            ).astype(BF16)

    def add(into, *terms):
        value = into[...].astype(F32)
        for ref, _ in terms:
            value += ref[...].astype(F32)
        into[...] = value.astype(BF16)

    def give(src, dst, device):
        n = sems.take()
        push(src, dst, n, device)
        return dst, n

    def wait_all(*terms):
        for ref, n in terms:
            arrive(ref, n)

    loads[2].wait()
    wd_move.wait()
    shared(0)
    down(0, 2)
    from_r_2 = give(yb.at[0, 2, 0], rh.at[1], left)
    shared(1)
    down(1, 2)
    from_y2 = give(yb.at[1, 2, 1], rh.at[0], across)
    from_r_q = give(yb.at[1, 2, 0, pl.ds(0, QUARTER)], rq.at[0], left)
    from_l_q = give(yb.at[1, 2, 0, pl.ds(QUARTER, QUARTER)], rq.at[1], right)
    down(1, 3)
    from_y_3 = give(yb.at[1, 3, 1], rh.at[2], across)
    down(1, 1)
    from_y_1 = give(yb.at[1, 1, 1], rh.at[3], across)
    wait_all(from_y2, from_r_q, from_l_q)
    add(yb.at[0, 2, 1], from_y2)
    from_l_2 = give(yb.at[0, 2, 1], rh.at[4], right)
    add(yb.at[1, 3, 0, pl.ds(0, QUARTER)], from_r_q)
    from_r_3 = give(yb.at[1, 3, 0], rh.at[5], left)
    add(yb.at[1, 1, 0, pl.ds(QUARTER, QUARTER)], from_l_q)
    from_l_1 = give(yb.at[1, 1, 0], rh.at[6], right)
    down(0, 1)
    last_l = [give(yb.at[0, 1, 0], rf.at[0, 0], right), None]
    down(1, 0)
    last_y = [None, give(yb.at[1, 0, 1], rf.at[1, 1], across)]
    down(0, 3)
    wait_all(from_r_2)
    add(yb.at[0, 3, 0], from_r_2)
    last_r = [give(yb.at[0, 3, 0], rf.at[2, 0], left), None]
    wait_all(from_y_3)
    add(yb.at[0, 3, 1], from_y_3)
    last_r[1] = give(yb.at[0, 3, 1], rf.at[2, 1], left)
    wait_all(from_y_1, from_l_2)
    add(yb.at[0, 1, 1], from_y_1, from_l_2)
    last_l[1] = give(yb.at[0, 1, 1], rf.at[0, 1], right)
    wait_all(from_r_3, from_l_1)
    add(yb.at[1, 0, 0], from_r_3, from_l_1)
    last_y[0] = give(yb.at[1, 0, 0], rf.at[1, 0], across)
    down(0, 0)

    r2_n = sems.take(16)
    r2_s = sems.take(16)

    far = lax.rem(zh + core, 2)

    def back(i, r):
        s = lax.rem(me8 + r, 8)
        device = kin(
            zl_=lax.div(s, 2), yh_=lax.rem(s, 2), core_=core if i == 0 else 1 - core, zh_=core
        )
        return pltpu.make_async_remote_copy(
            src_ref=r2s.at[i, s], dst_ref=r2.at[far, me8],
            send_sem=send.at[r2_s + 8 * i + r], recv_sem=recv.at[r2_n + far * 8 + me8],
            device_id=device, device_id_type=MESH,
        )

    for i in range(2):
        wait_all(last_l[i], last_r[i], last_y[i])
        value = (
            yb[0, 0, i].astype(F32)
            + rf[0, i].astype(F32)
            + rf[1, i].astype(F32)
            + rf[2, i].astype(F32)
        ).astype(BF16)
        for g in range(2):
            turned = dot(turn[...], fold(value[PACK * g : PACK * g + PACK]))
            r2s[i, 4 * g : 4 * g + 4] = turned.astype(BF16).reshape(4, PACK, 128)
        if i == 0:

            @pl.when(core == zh)
            def _():
                r2[0, me8] = r2s[0, me8]

            @pl.when(core != zh)
            def _():
                back(0, 0).start()

            pl.loop(1, 8)(lambda r: back(0, r).start())
        else:
            pl.loop(0, 8)(lambda r: back(1, r).start())

    def weighted(i):
        back_rows = r2[i].reshape(EXPERTS * PACK, 128)
        mixed = dot(cw[0], back_rows) + dot(cw[1], back_rows)
        return jnp.concatenate([mixed[128 * j : 128 * j + 128] for j in range(4)], axis=1)

    def returned(i, r):
        e = lax.rem(me8 + r, 8)
        arrive(r2.at[i, e], r2_n + 8 * i + e)

    pl.loop(1, 8)(lambda r: returned(0, r))

    @pl.when(core != zh)
    def _():
        returned(0, 0)

    mix = stream[...] + weighted(0)
    pl.loop(0, 8)(lambda r: returned(1, r))
    mix += weighted(1)
    out_ref[...] = mix.astype(BF16)

    for src, n in started:
        copy(src, src, n, mate).wait_send()

    @pl.loop(1, 16)
    def _(r):
        copy(gbuf.at[0], gbuf.at[0], d1_n + r, mate).wait_send()

    @pl.loop(0, 16)
    def _(r):
        copy(kv.at[0, 0, 0], kv.at[0, 0, 0], mate_n + r, mate).wait_send()

    for n in (*range(1, 8), *range(12, 16)):
        copy(kv.at[0, 0, 0], kv.at[0, 0, 0], kv_n + n, mate).wait_send()
    for n in range(4):
        copy(kv.at[0, 0, 0, early], kv.at[0, 0, 0, early], kv_n + 8 + n, mate).wait_send()
        copy(kv.at[0, 0, 0, late], kv.at[0, 0, 0, late], kv_half + n, mate).wait_send()

    @pl.loop(1, 8)
    def _(r):
        copy(ssq.at[0], ssq.at[0], ssq_n + r, mate).wait_send()

    @pl.when(core != zh)
    def _():
        back(0, 0).wait_send()

    pl.loop(1, 8)(lambda r: back(0, r).wait_send())
    pl.loop(0, 8)(lambda r: back(1, r).wait_send())


SEMS = 192


def body(
    query_rows, key_head_rows, value_head_rows, positions, residual, norm_gain, expert_ids,
    gate_fixed, w_gate, w_up, w_down,
):
    vmem = pl.BlockSpec(memory_space=pltpu.VMEM)
    hbm = pl.BlockSpec(memory_space=pl.ANY)
    return pl.pallas_call(
        kernel,
        out_shape=jax.ShapeDtypeStruct(residual.shape, BF16),
        in_specs=[vmem] * 8 + [hbm] * 3,
        out_specs=vmem,
        scratch_shapes=[
            pltpu.VMEM((2, 4, 4, 272, 128), BF16),
            pltpu.VMEM((8, 8, 128), F32),
            pltpu.VMEM((128, HALF), F32),
            pltpu.VMEM((EXPERTS * PACK, HALF), BF16),
            pltpu.VMEM((2, HALF, EXPERTS * PACK), BF16),
            pltpu.VMEM((4 * PACK, 4 * PACK), BF16),
            pltpu.VMEM((EXPERTS, PACK, 128), BF16),
            pltpu.VMEM((2, 8, PACK, 128), BF16),
            pltpu.VMEM((2, 2, 4, 2, ROWS, HALF), BF16),
            pltpu.VMEM(w_gate.shape[::-1], BF16),
            pltpu.VMEM(w_up.shape[::-1], BF16),
            pltpu.VMEM((2, w_down.shape[0], 2048), BF16),
            pltpu.VMEM((2, 2, ROWS, w_gate.shape[1]), F32),
            pltpu.VMEM((2, 2, ROWS, w_gate.shape[1]), F32),
            pltpu.VMEM((2, 2, 2, ROWS, w_gate.shape[1]), BF16),
            pltpu.VMEM((2, 4, 2, ROWS, HALF), BF16),
            pltpu.VMEM((2, QUARTER, HALF), BF16),
            pltpu.VMEM((7, ROWS, HALF), BF16),
            pltpu.VMEM((3, 2, ROWS, HALF), BF16),
            pltpu.VMEM((2, 8, PACK, 128), BF16),
            pltpu.VMEM((2, 8, PACK, 128), BF16),
            pltpu.SemaphoreType.DMA((SEMS,)),
            pltpu.SemaphoreType.DMA((SEMS,)),
            pltpu.SemaphoreType.DMA((3,)),
        ],
        compiler_params=pltpu.CompilerParams(
            collective_id=0, has_side_effects=True, vmem_limit_bytes=60 * 2**20
        ),
        cost_estimate=pl.CostEstimate(
            flops=14 * 10**9, bytes_accessed=12 * 10**6, transcendentals=3 * 10**6
        ),
    )(
        query_rows, key_head_rows, value_head_rows, expert_ids.T, gate_fixed.reshape(1, -1),
        positions.reshape(1, -1), residual, norm_gain.reshape(4, -1), w_gate.T, w_up.T, w_down,
    )


def solution(mesh):
    in_specs = (
        P("ctx", "head"),
        P("ctx", "head"),
        P("ctx", "head"),
        P("ctx"),
        P("ctx", "head"),
        P("head"),
        P("ctx", None),
        P("ctx"),
        P(None, ("ctx", "head")),
        P(None, ("ctx", "head")),
        P(("ctx", "head"), None),
    )
    out_specs = P("ctx", "head")
    return jax.shard_map(body, mesh=mesh, in_specs=in_specs, out_specs=out_specs, check_vma=False)
```
